128 devices in a mesh: dp: 8 (over y, x_hi), tensor: 16 (over z, x_lo, core).
Axes of the slice: x: 4 (x_hi: 2, x_lo: 2; x = x_hi * 2 + x_lo), y: 4, z: 4, core: 2. Of those that a mesh axis runs over, the one named last changes fastest.
Arguments:
- prefill_rows: bfloat16 [8192, 8192], P(('dp', 'tensor')), parts along dimension 0, may hold values from -6 to 6
- decode_rows: bfloat16 [256, 8192], P(('dp', 'tensor')), parts along dimension 0, may hold values from -6 to 6
- norm_gain: bfloat16 [8192], replicated, may hold values from 0.099609375 to 1.8984375
- w_query: bfloat16 [8192, 8192], P(None, 'tensor'), may hold values from -0.0625 to 0.0625
- w_key: bfloat16 [8192, 1024], P(None, 'tensor'), may hold values from -0.0625 to 0.0625
- w_value: bfloat16 [8192, 1024], P(None, 'tensor'), may hold values from -0.0625 to 0.0625
- w_out: bfloat16 [8192, 8192], P('tensor'), may hold values from -0.0625 to 0.0625
- prefix_keys: bfloat16 [8192, 1024], P('dp', 'tensor'), parts along dimension 0
- prefix_values: bfloat16 [8192, 1024], P('dp', 'tensor'), parts along dimension 0, may hold values from -6 to 6
- prefill_start: int32 [8], P('dp'), parts along dimension 0, may hold values from 512 to 1024
- cache_keys: bfloat16 [256, 512, 1024], P(('dp', 'tensor')), parts along dimension 0
- cache_values: bfloat16 [256, 512, 1024], P(('dp', 'tensor')), parts along dimension 0, may hold values from -6 to 6
- cache_lengths: int32 [256], P(('dp', 'tensor')), parts along dimension 0, may hold values from 1 to 512, as said below
Outputs:
- prefill_out: bfloat16 [8192, 8192], P(('dp', 'tensor')), parts along dimension 0
- decode_out: bfloat16 [256, 8192], P(('dp', 'tensor')), parts along dimension 0
The draws below stay inside these ranges and needn't reach their ends.
There are 8 independent parts, one for each index of `dp`. The reference program is written for one: setup_inputs(seed, part) draws one part's arguments, and reference() takes and returns one part's arrays. A program takes and returns all parts, laid end to end along the dimension named above; an argument that names none is the same for every part. Nothing has to cross between parts.
Inputs may be any that keep to these rules, and one draw needn't show every extreme that they name: `cache_lengths`: some decode row's cache holds exactly 512 positions.
All inputs are finite; a program needn't handle non-finite values.
Results may differ from the reference program's by a relative error of at most 0.024.
The reference program's roundings to bfloat16 on the way count: a program that leaves them out, or rounds other values in their place, can miss the bound.
Values may be sent and summed in bfloat16 or wider, within the bound.
No kernel may reach another device: no remote copies, remote signals or barrier semaphores. Data moves between devices by JAX's collectives and lax.ppermute only.
A program may use at most 192 MiB of HBM per device.

```python
import math
import jax
import jax.numpy as jnp
from jax import lax

D = 8192
HEADS = 64
KV_HEADS = 8
HEAD_DIM = 128
PREFILL = 1024
PREFIX = 1024
DEC_LEN = 512
DECODE = 32
N_TENSOR = 16


def draw_prefix_keys(key, part):
    key = jax.random.fold_in(key, 11)
    shape = (PREFIX, KV_HEADS * HEAD_DIM)
    base = jax.random.normal(key, shape, jnp.float32)
    return base.astype(jnp.bfloat16)


def draw_cache_keys(key, part):
    key = jax.random.fold_in(key, 13)
    shape = (DECODE, DEC_LEN, KV_HEADS * HEAD_DIM)
    base = jax.random.normal(key, shape, jnp.float32)
    return base.astype(jnp.bfloat16)


def draw_cache_lengths(key, part):
    key = jax.random.fold_in(key, 17)
    lengths = jax.random.randint(key, (DECODE,), 1, DEC_LEN + 1)
    chosen = jax.random.randint(jax.random.fold_in(key, 1), (), 0, DECODE)
    return jnp.where(jnp.arange(DECODE, dtype=jnp.int32) == chosen, DEC_LEN, lengths).astype(jnp.int32)


def block_levels(stream_key, dims, cuts, low, high):
    level = 1.0
    for axis_at, blocks in cuts:
        steps = jax.random.uniform(jax.random.fold_in(jax.random.fold_in(stream_key, 6), axis_at), (blocks,), jnp.float32, low / len(cuts), high / len(cuts))
        level = level * jnp.repeat(jnp.exp(steps), dims[axis_at] // blocks).reshape((-1,) + (1,) * (len(dims) - 1 - axis_at))
    return level


def gaussian(key, dims, width, bound, cuts=(), held_as=jnp.bfloat16):
    level = block_levels(key, dims, cuts, -0.22, 0.18) if cuts else 1.0
    drawn = jax.random.normal(key, dims, jnp.float32) * width * level
    return jnp.minimum(jnp.maximum(drawn, -bound), bound).astype(held_as)


def setup_inputs(seed: int = 0, part: int = 0) -> dict:
    key_of = jax.random.split(jax.random.key(seed), 14)
    own_keys = jax.random.split(jax.random.fold_in(key_of[13], part), 14)
    return {
        "prefill_rows": gaussian(own_keys[0], (PREFILL, D), 1.0, 6.0, ((0, 16),)),
        "decode_rows": gaussian(own_keys[1], (DECODE, D), 1.0, 6.0, ((0, 16),)),
        "norm_gain": jnp.clip(1.0 + 0.18 * jax.random.normal(key_of[2], (D,), jnp.float32), 0.099609375, 1.8984375).astype(jnp.bfloat16),
        "w_query": gaussian(key_of[3], (D, HEADS * HEAD_DIM), D ** -0.5, 0.0625, ((1, 16),)),
        "w_key": gaussian(key_of[4], (D, KV_HEADS * HEAD_DIM), D ** -0.5, 0.0625, ((1, 16),)),
        "w_value": gaussian(key_of[5], (D, KV_HEADS * HEAD_DIM), D ** -0.5, 0.0625, ((1, 16),)),
        "w_out": gaussian(key_of[6], (HEADS * HEAD_DIM, D), (HEADS * HEAD_DIM) ** -0.5, 0.0625, ((0, 16),)),
        "prefix_keys": draw_prefix_keys(jax.random.fold_in(jax.random.fold_in(key_of[13], part), 71), part),
        "prefix_values": gaussian(own_keys[8], (PREFIX, KV_HEADS * HEAD_DIM), 1.0, 6.0, ((1, 16),)),
        "prefill_start": jax.random.randint(own_keys[9], (1,), PREFIX // 2, PREFIX + 1).astype(jnp.int32),
        "cache_keys": draw_cache_keys(jax.random.fold_in(jax.random.fold_in(key_of[13], part), 71), part),
        "cache_values": gaussian(own_keys[11], (DECODE, DEC_LEN, KV_HEADS * HEAD_DIM), 1.0, 6.0, ((0, 16),)),
        "cache_lengths": draw_cache_lengths(jax.random.fold_in(jax.random.fold_in(key_of[13], part), 71), part),
    }


def rms_norm(rows, gain):
    widened = rows.astype(jnp.float32)
    mean_sq = lax.optimization_barrier(jnp.mean(widened * widened, axis=-1, keepdims=True))
    return (widened * lax.rsqrt(mean_sq + 1e-05) * gain.astype(jnp.float32)).astype(jnp.bfloat16)

def rotate(values, positions):
    half_dim = values.shape[-1] // 2
    frequency = jnp.exp(jnp.arange(half_dim, dtype=jnp.float32) * (-2.0 * math.log(500000.0) / values.shape[-1]))
    angles = positions[..., None] * frequency
    cosine = jnp.cos(angles)
    sine_part = jnp.sin(angles)
    widened = values.astype(jnp.float32)
    first_half = widened[..., :half_dim]
    second_half = widened[..., half_dim:]
    return jnp.concatenate([first_half * cosine - second_half * sine_part, second_half * cosine + first_half * sine_part], -1).astype(jnp.bfloat16)

def project(normed, weight):
    return jnp.dot(normed, weight, preferred_element_type=jnp.float32).astype(jnp.bfloat16)

def as_float(values):
    return lax.optimization_barrier(values).astype(jnp.float32)

def out_project(attn, w_out):
    rows = attn.shape[0]
    per_group = HEADS * HEAD_DIM // N_TENSOR
    groups = attn.reshape(rows, N_TENSOR, per_group).transpose(1, 0, 2)
    weights = w_out.reshape(N_TENSOR, per_group, D)

    def add_term(carry, pair):
        return (carry + as_float(jnp.dot(pair[0], pair[1], preferred_element_type=jnp.float32).astype(jnp.bfloat16)), None)
    total, unused = lax.scan(add_term, jnp.zeros((rows, D), jnp.float32), (groups, weights))
    return total.astype(jnp.bfloat16)

def reference(prefill_rows, decode_rows, norm_gain, w_query, w_key, w_value, w_out, prefix_keys, prefix_values, prefill_start, cache_keys, cache_values, cache_lengths):
    group_size = HEADS // KV_HEADS
    score_scale = HEAD_DIM ** (-0.5)
    offset = prefill_start[0]
    normed_pre = rms_norm(prefill_rows, norm_gain)
    normed_dec = rms_norm(decode_rows, norm_gain)
    pre_pos = (offset + jnp.arange(PREFILL, dtype=jnp.int32)).astype(jnp.float32)
    q_pre = rotate(project(normed_pre, w_query).reshape(PREFILL, HEADS, HEAD_DIM), pre_pos[:, None])
    k_pre = rotate(project(normed_pre, w_key).reshape(PREFILL, KV_HEADS, HEAD_DIM), pre_pos[:, None])
    v_pre = project(normed_pre, w_value).reshape(PREFILL, KV_HEADS, HEAD_DIM)
    all_keys = jnp.concatenate([prefix_keys.reshape(PREFIX, KV_HEADS, HEAD_DIM), k_pre], 0)
    all_values = jnp.concatenate([prefix_values.reshape(PREFIX, KV_HEADS, HEAD_DIM), v_pre], 0)
    row_index = jnp.arange(PREFILL, dtype=jnp.int32)
    allowed = jnp.concatenate([jnp.broadcast_to(jnp.arange(PREFIX, dtype=jnp.int32)[None, :] < offset, (PREFILL, PREFIX)), row_index[None, :] <= row_index[:, None]], 1)

    def one_group(kv_group):
        queries = lax.dynamic_slice_in_dim(q_pre, kv_group * group_size, group_size, 1).astype(jnp.float32)
        keys_here = lax.dynamic_index_in_dim(all_keys, kv_group, 1, keepdims=False).astype(jnp.float32)
        values_here = lax.dynamic_index_in_dim(all_values, kv_group, 1, keepdims=False).astype(jnp.float32)
        scores = jnp.einsum('qhd,kd->hqk', queries, keys_here) * score_scale
        scores = jnp.where(allowed[None], scores, -jnp.inf)
        probs = as_float(jax.nn.softmax(scores, axis=-1).astype(jnp.bfloat16))
        return jnp.einsum('hqk,kd->qhd', probs, values_here).astype(jnp.bfloat16)
    blocks = lax.map(one_group, jnp.arange(KV_HEADS, dtype=jnp.int32))
    attn_pre = blocks.transpose(1, 0, 2, 3).reshape(PREFILL, HEADS * HEAD_DIM)
    dec_pos = cache_lengths.astype(jnp.float32)
    q_dec = rotate(project(normed_dec, w_query).reshape(DECODE, HEADS, HEAD_DIM), dec_pos[:, None])
    q_dec = q_dec.reshape(DECODE, KV_HEADS, group_size, HEAD_DIM).astype(jnp.float32)
    k_dec = rotate(project(normed_dec, w_key).reshape(DECODE, KV_HEADS, HEAD_DIM), dec_pos[:, None]).astype(jnp.float32)
    v_dec = project(normed_dec, w_value).reshape(DECODE, KV_HEADS, HEAD_DIM).astype(jnp.float32)
    cached_k = cache_keys.reshape(DECODE, DEC_LEN, KV_HEADS, HEAD_DIM).astype(jnp.float32)
    cached_v = cache_values.reshape(DECODE, DEC_LEN, KV_HEADS, HEAD_DIM).astype(jnp.float32)
    old_scores = jnp.einsum('rgjd,rlgd->rgjl', q_dec, cached_k) * score_scale
    valid = jnp.arange(DEC_LEN, dtype=jnp.int32)[None, :] < cache_lengths[:, None]
    old_scores = jnp.where(valid[:, None, None, :], old_scores, -jnp.inf)
    own_score = jnp.einsum('rgjd,rgd->rgj', q_dec, k_dec) * score_scale
    scores = jnp.concatenate([old_scores, own_score[..., None]], -1)
    probs = as_float(jax.nn.softmax(scores, axis=-1).astype(jnp.bfloat16))
    mixed = jnp.einsum('rgjl,rlgd->rgjd', probs[..., :DEC_LEN], cached_v) + probs[..., DEC_LEN:] * v_dec[:, :, None, :]
    attn_dec = mixed.astype(jnp.bfloat16).reshape(DECODE, HEADS * HEAD_DIM)
    return (out_project(attn_pre, w_out), out_project(attn_dec, w_out))
```

```python
import functools
import math

import jax
import jax.numpy as jnp
from jax import lax
from jax.experimental import pallas as pl
from jax.experimental.pallas import tpu as pltpu
from jax.sharding import PartitionSpec as P

HEAD_DIM = 128
RING = 4
BF16 = jnp.bfloat16
F32 = jnp.float32
NT = (((1,), (1,)), ((), ()))


def route(move):
    pairs = []
    for z in range(RING):
        for x in range(2):
            for c in range(2):
                z2, x2, c2 = move(z, x, c)
                pairs.append(((z * 2 + x) * 2 + c, ((z2 % RING) * 2 + x2) * 2 + c2))
    return pairs


UP = route(lambda z, x, c: (z + 1, x, c))
DOWN = route(lambda z, x, c: (z - 1, x, c))
SIDE = route(lambda z, x, c: (z, 1 - x, c))
CORE = route(lambda z, x, c: (z, x, 1 - c))
SAME_CORE = [list(range(0, 4 * RING, 2)), list(range(1, 4 * RING, 2))]


def up(block):
    return lax.ppermute(block, "tensor", UP)


def down(block):
    return lax.ppermute(block, "tensor", DOWN)


def side(block):
    return lax.ppermute(block, "tensor", SIDE)


def swap(block):
    return lax.ppermute(block, "tensor", CORE)


def exchange(block):
    return lax.all_to_all(
        block, "tensor", split_axis=0, concat_axis=0, axis_index_groups=SAME_CORE, tiled=True
    )


def rms_norm(rows, gain):
    widened = rows.astype(F32)
    mean_sq = jnp.mean(widened * widened, axis=-1, keepdims=True)
    return (widened * lax.rsqrt(mean_sq + 1e-05) * gain.astype(F32)).astype(BF16)


def norm_kernel(a_ref, b_ref, gain_ref, a_out, b_out):
    gain = gain_ref[...]
    a_out[...] = rms_norm(a_ref[...], gain)
    b_out[...] = rms_norm(b_ref[...], gain)


def norm_halves(rows, gain):
    count, width = rows.shape
    half = count // 2
    step = 16
    steps = half // step
    return pl.pallas_call(
        norm_kernel,
        grid=(steps,),
        in_specs=[
            pl.BlockSpec((step, width), lambda i: (i, 0)),
            pl.BlockSpec((step, width), lambda i: (i + steps, 0)),
            pl.BlockSpec((1, width), lambda i: (0, 0)),
        ],
        out_specs=[pl.BlockSpec((step, width), lambda i: (i, 0))] * 2,
        out_shape=[jax.ShapeDtypeStruct((half, width), BF16)] * 2,
        name="norm_halves",
    )(rows, rows, gain.reshape(1, width))


def turn(values, cosine, signed_sine):
    widened = values.astype(F32)
    return (widened * cosine + pltpu.roll(widened, 64, 1) * signed_sine).astype(BF16)


def project_kernel(pieces, turned, core_ref, *refs):
    xs = refs[:pieces]
    wq_own, wq_other, wkv_own, wkv_other, cos_ref, sin_ref, q_out, kv_out, acc = refs[pieces:]
    step = pl.program_id(0)
    x = jnp.concatenate([r[...] for r in xs], axis=0) if pieces > 1 else xs[0][...]
    own_low = core_ref[0] == 0
    own, other = wkv_own[...], wkv_other[...]
    low = jnp.where(own_low, own, other)
    high = jnp.where(own_low, other, own)
    wkv = jnp.concatenate([low[:64], high[:64], low[64:], high[64:]], axis=0)
    cols = wq_own.shape[1]

    @pl.when(step == 0)
    def _():
        acc[...] = jnp.zeros_like(acc)

    acc[:, :cols] += jnp.dot(x, wq_own[...], preferred_element_type=F32)
    acc[:, cols : 2 * cols] += jnp.dot(x, wq_other[...], preferred_element_type=F32)
    acc[:, 2 * cols :] += lax.dot_general(x, wkv, NT, preferred_element_type=F32)

    @pl.when(step == pl.num_programs(0) - 1)
    def _():
        cosine, sine = cos_ref[...], sin_ref[...]
        total = acc.shape[0]
        for head in range(2 * cols // HEAD_DIM):
            at = slice(head * HEAD_DIM, (head + 1) * HEAD_DIM)
            raw = acc[:, at].astype(BF16)
            q_out[:turned, at] = turn(raw[:turned], cosine, sine)
            if total > turned:
                q_out[turned:, at] = raw[turned:]
        raw = acc[:, 2 * cols :].astype(BF16)
        kv_out[:turned, :HEAD_DIM] = turn(raw[:turned, :HEAD_DIM], cosine, sine)
        kv_out[:turned, HEAD_DIM:] = raw[:turned, HEAD_DIM:]
        if total > turned:
            kv_out[turned:, :] = raw[turned:]


def project(xs, turned, core, wq_own, wq_other, wkv_own, wkv_other, cosine, sine, name):
    total = sum(x.shape[0] for x in xs)
    width = xs[0].shape[1]
    cols = wq_own.shape[1]
    deep = 1024
    flops = 2 * total * width * (2 * cols + 256)
    return pl.pallas_call(
        functools.partial(project_kernel, len(xs), turned),
        grid_spec=pltpu.PrefetchScalarGridSpec(
            num_scalar_prefetch=1,
            grid=(width // deep,),
            in_specs=[pl.BlockSpec((x.shape[0], deep), lambda k, s: (0, k)) for x in xs]
            + [
                pl.BlockSpec((deep, cols), lambda k, s: (k, 0)),
                pl.BlockSpec((deep, cols), lambda k, s: (k, 0)),
                pl.BlockSpec((128, deep), lambda k, s: (0, k)),
                pl.BlockSpec((128, deep), lambda k, s: (0, k)),
                pl.BlockSpec((turned, HEAD_DIM), lambda k, s: (0, 0)),
                pl.BlockSpec((turned, HEAD_DIM), lambda k, s: (0, 0)),
            ],
            out_specs=[
                pl.BlockSpec((total, 2 * cols), lambda k, s: (0, 0)),
                pl.BlockSpec((total, 256), lambda k, s: (0, 0)),
            ],
            scratch_shapes=[pltpu.VMEM((total, 2 * cols + 256), F32)],
        ),
        out_shape=[
            jax.ShapeDtypeStruct((total, 2 * cols), BF16),
            jax.ShapeDtypeStruct((total, 256), BF16),
        ],
        compiler_params=pltpu.CompilerParams(vmem_limit_bytes=32 << 20),
        cost_estimate=pl.CostEstimate(
            flops=flops, bytes_accessed=2 * (total * width + width * (2 * cols + 256)), transcendentals=0
        ),
        name=name,
    )(core, *xs, wq_own, wq_other, wkv_own, wkv_other, cosine, sine)


def attend_kernel(blocks, prefix, spec_ref, q_ref, pk_ref, pv_ref, *refs):
    own_refs, other_refs = refs[:2], refs[2:4]
    out_ref, k_all, v_all = refs[4:]
    first = jnp.logical_and(pl.program_id(0) == 0, pl.program_id(1) == 0)
    rows = out_ref.shape[0]

    @pl.when(first)
    def _():
        k_all[:prefix] = pk_ref[...]
        v_all[:prefix, :HEAD_DIM] = pv_ref[...]
        v_all[:, HEAD_DIM:] = jnp.ones((v_all.shape[0], HEAD_DIM), BF16)
        for j in range(2 * RING):
            place = spec_ref[1 + j]
            for refs_here, at in ((own_refs, place), (other_refs, place ^ 1)):
                block = refs_here[j // RING][(j % RING) * rows : (j % RING + 1) * rows, :]
                here = pl.ds(pl.multiple_of(prefix + at * rows, rows), rows)
                k_all[here, :] = block[:, :HEAD_DIM]
                v_all[here, :HEAD_DIM] = block[:, HEAD_DIM:]

    place = spec_ref[1 + 2 * RING + pl.program_id(0)]
    start = spec_ref[0]
    heads = q_ref.shape[1] // HEAD_DIM
    group = 4 * rows
    for level in range(RING):

        @pl.when(place // 4 == level)
        def _():
            keys = prefix + group * (level + 1)
            q = jnp.concatenate(
                [q_ref[:, h * HEAD_DIM : (h + 1) * HEAD_DIM] for h in range(heads)], axis=0
            )
            scores = lax.dot_general(q, k_all[:keys, :], NT, preferred_element_type=F32) * (
                HEAD_DIM**-0.5
            )
            half = prefix // 2
            last = keys - group
            col = lax.broadcasted_iota(jnp.int32, (heads * rows, half), 1) + half
            late = jnp.where(col < start, scores[:, half:prefix], -jnp.inf)
            row = lax.broadcasted_iota(jnp.int32, (heads * rows, group), 0) % rows
            own_col = lax.broadcasted_iota(jnp.int32, (heads * rows, group), 1)
            diag = jnp.where(
                own_col <= row + (place % 4) * rows, scores[:, last:], -jnp.inf
            )
            parts = [scores[:, :half], late]
            if last > prefix:
                parts.append(scores[:, prefix:last])
            parts.append(diag)
            top = functools.reduce(
                jnp.maximum, [jnp.max(p, axis=1, keepdims=True) for p in parts]
            )
            probs = jnp.concatenate([jnp.exp(p - top).astype(BF16) for p in parts], axis=1)
            mixed = jnp.dot(probs, v_all[:keys, :], preferred_element_type=F32)
            out = (mixed[:, :HEAD_DIM] / mixed[:, HEAD_DIM:]).astype(BF16)
            for h in range(heads):
                out_ref[:, h * HEAD_DIM : (h + 1) * HEAD_DIM] = out[h * rows : (h + 1) * rows]


def attend(spec, q, prefix_k, prefix_v, own, other, rows, name):
    prefix = prefix_k.shape[0]
    width = q.shape[1]
    blocks = RING
    total = prefix + 4 * RING * rows

    def whole(a):
        return pl.BlockSpec(a.shape, lambda i, g, s: (0, 0))

    return pl.pallas_call(
        functools.partial(attend_kernel, blocks, prefix),
        grid_spec=pltpu.PrefetchScalarGridSpec(
            num_scalar_prefetch=1,
            grid=(blocks, 2),
            in_specs=[
                pl.BlockSpec((rows, width // 2), lambda i, g, s: (i, g)),
                whole(prefix_k),
                whole(prefix_v),
            ]
            + [whole(a) for a in own + other],
            out_specs=pl.BlockSpec((rows, width // 2), lambda i, g, s: (i, g)),
            scratch_shapes=[
                pltpu.VMEM((total, HEAD_DIM), BF16),
                pltpu.VMEM((total, 2 * HEAD_DIM), BF16),
            ],
        ),
        out_shape=jax.ShapeDtypeStruct((blocks * rows, width), BF16),
        compiler_params=pltpu.CompilerParams(vmem_limit_bytes=48 << 20),
        cost_estimate=pl.CostEstimate(
            flops=4 * blocks * rows * width * total,
            bytes_accessed=2 * (2 * blocks * rows * width + 3 * total * HEAD_DIM),
            transcendentals=blocks * rows * width // HEAD_DIM * total,
        ),
        name=name,
    )(spec, q, prefix_k, prefix_v, *own, *other)


def emit_kernel(inputs, sizes, *refs):
    xs, (own_ref, other_ref), outs = refs[:inputs], refs[inputs : inputs + 2], refs[inputs + 2 :]
    half = own_ref.shape[0]
    x = jnp.concatenate([r[...] for r in xs], axis=0) if inputs > 1 else xs[0][...]
    partial = jnp.dot(x[:, :half], own_ref[...], preferred_element_type=F32) + jnp.dot(
        x[:, half:], other_ref[...], preferred_element_type=F32
    )
    partial = partial.astype(BF16)
    at = 0
    for out, size in zip(outs, sizes):
        out[...] = partial[at : at + size]
        at += size


def emit(xs, own, other, sizes, name):
    total = sum(x.shape[0] for x in xs)
    half, width = own.shape
    wide = 1024
    return pl.pallas_call(
        functools.partial(emit_kernel, len(xs), tuple(sizes)),
        grid=(width // wide,),
        in_specs=[pl.BlockSpec(x.shape, lambda n: (0, 0)) for x in xs]
        + [pl.BlockSpec((half, wide), lambda n: (0, n))] * 2,
        out_specs=[pl.BlockSpec((size, wide), lambda n: (0, n)) for size in sizes],
        out_shape=[jax.ShapeDtypeStruct((size, width), BF16) for size in sizes],
        compiler_params=pltpu.CompilerParams(vmem_limit_bytes=32 << 20),
        cost_estimate=pl.CostEstimate(
            flops=4 * total * half * width,
            bytes_accessed=2 * (total * (2 * half + width) + 2 * half * width),
            transcendentals=0,
        ),
        name=name,
    )(*xs, own, other)


def frequencies():
    half_dim = HEAD_DIM // 2
    return jnp.exp(
        jnp.arange(half_dim, dtype=F32) * (-2.0 * math.log(500000.0) / HEAD_DIM)
    )


def tables(positions):
    angles = positions.astype(F32)[:, None] * frequencies()
    cosine, sine = jnp.cos(angles), jnp.sin(angles)
    return jnp.concatenate([cosine, cosine], 1), jnp.concatenate([-sine, sine], 1)


def rotate(values, positions):
    half_dim = values.shape[-1] // 2
    angles = positions[..., None] * frequencies()
    cosine, sine = jnp.cos(angles), jnp.sin(angles)
    widened = values.astype(F32)
    first, second = widened[..., :half_dim], widened[..., half_dim:]
    return jnp.concatenate(
        [first * cosine - second * sine, second * cosine + first * sine], -1
    ).astype(BF16)


def decode_attend(queries, new_keys, new_values, cached_keys, cached_values, lengths):
    rows, kv_heads, group_size, _ = queries.shape
    scale = HEAD_DIM**-0.5
    positions = lengths.astype(F32)
    q_rot = rotate(queries, positions[:, None, None])
    k_rot = rotate(new_keys, positions[:, None])
    span = cached_keys.shape[1]
    cache_k = cached_keys.reshape(rows, span, kv_heads, HEAD_DIM)
    cache_v = cached_values.reshape(rows, span, kv_heads, HEAD_DIM)
    old = jnp.einsum("rgjd,rlgd->rgjl", q_rot, cache_k, preferred_element_type=F32) * scale
    valid = jnp.arange(span, dtype=jnp.int32)[None, :] < lengths[:, None]
    old = jnp.where(valid[:, None, None, :], old, -jnp.inf)
    own = jnp.einsum("rgjd,rgd->rgj", q_rot, k_rot, preferred_element_type=F32) * scale
    top = jnp.maximum(jnp.max(old, axis=-1), own)
    old_weights = jnp.exp(old - top[..., None])
    own_weight = jnp.exp(own - top)
    total = jnp.sum(old_weights, axis=-1) + own_weight
    old_probs = (old_weights / total[..., None]).astype(BF16)
    own_prob = (own_weight / total).astype(BF16)
    mixed = jnp.einsum("rgjl,rlgd->rgjd", old_probs, cache_v, preferred_element_type=F32)
    mixed = mixed + own_prob.astype(F32)[..., None] * new_values.astype(F32)[:, :, None, :]
    return mixed.astype(BF16)


def add(*terms):
    return functools.reduce(lambda a, b: a + b, [t.astype(F32) for t in terms]).astype(BF16)


def shards(
    prefill_rows,
    decode_rows,
    norm_gain,
    w_query,
    w_key,
    w_value,
    w_out,
    prefix_keys,
    prefix_values,
    prefill_start,
    cache_keys,
    cache_values,
    cache_lengths,
):
    index = lax.axis_index("tensor")
    core, chip_x, chip_z = index & 1, (index >> 1) & 1, index >> 2
    rows = prefill_rows.shape[0]
    dec = decode_rows.shape[0]
    chips = 2 * RING
    half = rows // 2
    quarter = half // 2
    width = prefill_rows.shape[1]

    a0, b0 = norm_halves(prefill_rows, norm_gain)
    a1, b1 = side(a0), side(b0)
    a3, b3 = up(a0), up(b0)
    a2, b2 = down(a0), down(b0)
    dec_own = rms_norm(decode_rows, norm_gain)
    dec_rows = exchange(
        jnp.broadcast_to(dec_own[None], (chips, dec, width)).reshape(chips * dec, width)
    )
    wkv_own = jnp.concatenate([w_key.T, w_value.T], 0)
    wkv_other = swap(wkv_own)
    wq_other = swap(w_query)
    pkv_own = jnp.concatenate([prefix_keys.T, prefix_values.T], 0)
    pkv_other = swap(pkv_own)
    wo_other = swap(w_out)

    a6, b6 = up(a3), down(b2)
    a5, a4 = up(a1), down(a1)
    b4, b5 = side(b2), side(b3)
    a7 = [up(a5[:quarter]), down(a4[quarter:])]
    b7 = side(b6)

    low = jnp.where(core == 0, pkv_own, pkv_other)
    high = jnp.where(core == 0, pkv_other, pkv_own)
    kv_cols = prefix_keys.shape[1]
    prefix_k = jnp.concatenate([low[:kv_cols], high[:kv_cols]], 0).T
    prefix_v = jnp.concatenate([low[kv_cols:], high[kv_cols:]], 0).T

    places = []
    for z_off, flip in ((0, 0), (0, 1), (1, 0), (3, 0), (1, 1), (3, 1), (2, 0), (2, 1)):
        places.append((((chip_z + z_off) % RING) * 2 + (chip_x ^ flip)) * 2 + core)
    start = prefill_start[0]
    offsets = jnp.arange(rows, dtype=jnp.int32)
    near_pos = jnp.concatenate([start + p * rows + offsets for p in places[:4]])
    far_pos = jnp.concatenate([start + p * rows + offsets for p in places[4:]])
    near_cos, near_sin = tables(near_pos)
    far_cos, far_sin = tables(far_pos)
    core_spec = core.reshape(1).astype(jnp.int32)

    weights = (w_query, wq_other, wkv_own, wkv_other)
    turned = 4 * rows
    q_near, kv_near = project(
        [a0, b0, a1, b1, a2, b2, a3, b3, dec_rows],
        turned,
        core_spec,
        *weights,
        near_cos,
        near_sin,
        "project_near",
    )
    dec_qkv = jnp.concatenate([q_near[turned:], kv_near[turned:]], 1)
    q_near, kv_near = q_near[:turned], kv_near[:turned]
    kv_near_other = swap(kv_near)
    q_far, kv_far = project(
        [a4, b4, a5, b5, a6, b6, *a7, b7],
        turned,
        core_spec,
        *weights,
        far_cos,
        far_sin,
        "project_far",
    )
    kv_far_other = swap(kv_far)

    q_cols = 2 * w_query.shape[1]
    mine = exchange(dec_qkv).reshape(chips, dec, -1).transpose(1, 0, 2)
    dec_attn = decode_attend(
        mine[:, :, :q_cols].reshape(dec, chips, q_cols // HEAD_DIM, HEAD_DIM),
        mine[:, :, q_cols : q_cols + HEAD_DIM],
        mine[:, :, q_cols + HEAD_DIM :],
        cache_keys,
        cache_values,
        cache_lengths,
    )
    dec_attn = exchange(
        dec_attn.reshape(dec, chips, q_cols).transpose(1, 0, 2).reshape(chips * dec, q_cols)
    )

    own, other = [kv_near, kv_far], [kv_near_other, kv_far_other]
    head = [start] + places
    far_spec = jnp.stack(head + places[4:]).astype(jnp.int32)
    near_spec = jnp.stack(head + places[:4]).astype(jnp.int32)
    attn_far = attend(far_spec, q_far, prefix_k, prefix_v, own, other, rows, "attend_far")
    pieces = [half] * 6 + [quarter, quarter, half]
    p4a, p4b, p5a, p5b, p6a, p6b, p7lo, p7hi, p7b = emit(
        [attn_far], w_out, wo_other, pieces, "emit_far"
    )
    r6b = side(p7b)
    r4hi, r5lo = up(p7hi), down(p7lo)
    attn_near = attend(near_spec, q_near, prefix_k, prefix_v, own, other, rows, "attend_near")
    p0a, p0b, p1a, p1b, p2a, p2b, p3a, p3b, pdec = emit(
        [attn_near, dec_attn], w_out, wo_other, [half] * 8 + [chips * dec], "emit_near"
    )
    p4a = jnp.concatenate([p4a[:quarter], add(p4a[quarter:], r4hi)], 0)
    p5a = jnp.concatenate([add(p5a[:quarter], r5lo), p5a[quarter:]], 0)
    r1a_up, r1a_down = up(p4a), down(p5a)
    r2b_side, r3b_side = side(p4b), side(p5b)
    r3a = down(p6a)
    r2b = up(add(p6b, r6b))
    r0a_side = side(add(p1a, r1a_up, r1a_down))
    r0b_side = side(p1b)
    r0a_up, r0b_up = up(p2a), up(add(p2b, r2b_side, r2b))
    r0a_down, r0b_down = down(add(p3a, r3a)), down(add(p3b, r3b_side))
    prefill_out = jnp.concatenate(
        [add(p0a, r0a_side, r0a_up, r0a_down), add(p0b, r0b_side, r0b_up, r0b_down)], 0
    )
    dec_parts = exchange(pdec).reshape(chips, dec, width)
    decode_out = jnp.sum(dec_parts.astype(F32), axis=0).astype(BF16)
    return (prefill_out, decode_out)


def solution(mesh):
    in_specs = (
        P(("dp", "tensor"), None),
        P(("dp", "tensor"), None),
        P(),
        P(None, "tensor"),
        P(None, "tensor"),
        P(None, "tensor"),
        P("tensor", None),
        P("dp", "tensor"),
        P("dp", "tensor"),
        P("dp"),
        P(("dp", "tensor"), None, None),
        P(("dp", "tensor"), None, None),
        P(("dp", "tensor")),
    )
    out_specs = (P(("dp", "tensor"), None), P(("dp", "tensor"), None))
    return jax.shard_map(shards, mesh=mesh, in_specs=in_specs, out_specs=out_specs, check_vma=False)
```

```python
import functools
import math

import jax
import jax.numpy as jnp
from jax import lax
from jax.experimental import pallas as pl
from jax.experimental.pallas import tpu as pltpu
from jax.sharding import PartitionSpec as P

HEAD_DIM = 128
RING = 4
BF16 = jnp.bfloat16
F32 = jnp.float32
NT = (((1,), (1,)), ((), ()))
WIDE = 1024


def route(move):
    pairs = []
    for z in range(RING):
        for x in range(2):
            for c in range(2):
                z2, x2, c2 = move(z, x, c)
                pairs.append(((z * 2 + x) * 2 + c, ((z2 % RING) * 2 + x2) * 2 + c2))
    return pairs


UP = route(lambda z, x, c: (z + 1, x, c))
DOWN = route(lambda z, x, c: (z - 1, x, c))
SIDE = route(lambda z, x, c: (z, 1 - x, c))
CORE = route(lambda z, x, c: (z, x, 1 - c))
SAME_CORE = [list(range(0, 4 * RING, 2)), list(range(1, 4 * RING, 2))]


def up(block):
    return lax.ppermute(block, "tensor", UP)


def down(block):
    return lax.ppermute(block, "tensor", DOWN)


def side(block):
    return lax.ppermute(block, "tensor", SIDE)


def swap(block):
    return lax.ppermute(block, "tensor", CORE)


def together(*arrays):
    return lax.optimization_barrier(arrays)


def exchange(block):
    return lax.all_to_all(
        block, "tensor", split_axis=0, concat_axis=0, axis_index_groups=SAME_CORE, tiled=True
    )


def rms_norm(rows, gain):
    widened = rows.astype(F32)
    mean_sq = jnp.mean(widened * widened, axis=-1, keepdims=True)
    return (widened * lax.rsqrt(mean_sq + 1e-05) * gain.astype(F32)).astype(BF16)


def norm_kernel(x_ref, gain_ref, out_ref):
    out_ref[...] = rms_norm(x_ref[...], gain_ref[...])


def norm_rows(rows, gain):
    count, width = rows.shape
    step = 16
    return pl.pallas_call(
        norm_kernel,
        grid=(count // step,),
        in_specs=[
            pl.BlockSpec((step, width), lambda i: (i, 0)),
            pl.BlockSpec((1, width), lambda i: (0, 0)),
        ],
        out_specs=pl.BlockSpec((step, width), lambda i: (i, 0)),
        out_shape=jax.ShapeDtypeStruct((count, width), BF16),
        name="norm_rows",
    )(rows, gain.reshape(1, width))


def turn(values, cosine, signed_sine):
    widened = values.astype(F32)
    return (widened * cosine + pltpu.roll(widened, 64, 1) * signed_sine).astype(BF16)


def project_kernel(inputs, pieces, cuts, turned, core_ref, *refs):
    xs = refs[:inputs]
    sources, (cos_ref, sin_ref), outs = refs[inputs : inputs + 4], refs[inputs + 4 : inputs + 6], refs[inputs + 6 :]
    q_out, kv_out = outs[:2]
    acc, rows, wq_own, wq_other, wkv_own, wkv_other, sems = outs[-7:]
    dec_out = outs[2] if len(outs) > 9 else None
    cols = wq_own.shape[1]

    def copies(k):
        at = pl.ds(cuts[k], cuts[k + 1] - cuts[k])
        low = 0
        for n, (i, first, size) in enumerate(pieces):
            yield pltpu.make_async_copy(
                xs[i].at[pl.ds(first, size), at], rows.at[pl.ds(low, size), at], sems.at[n, k]
            )
            low += size
        n = len(pieces)
        yield pltpu.make_async_copy(sources[0].at[at, :], wq_own.at[at, :], sems.at[n, k])
        yield pltpu.make_async_copy(sources[1].at[at, :], wq_other.at[at, :], sems.at[n + 1, k])
        yield pltpu.make_async_copy(sources[2].at[:, at], wkv_own.at[:, at], sems.at[n + 2, k])
        yield pltpu.make_async_copy(sources[3].at[:, at], wkv_other.at[:, at], sems.at[n + 3, k])

    steps = len(cuts) - 1
    for k in range(steps):
        for copy in copies(k):
            copy.start()
    own_low = core_ref[0] == 0
    for k in range(steps):
        at = slice(cuts[k], cuts[k + 1])
        for copy in copies(k):
            copy.wait()
        x = rows[:, at]
        own, other = wkv_own[:, at], wkv_other[:, at]
        low = jnp.where(own_low, own, other)
        high = jnp.where(own_low, other, own)
        wkv = jnp.concatenate([low[:64], high[:64], low[64:], high[64:]], axis=0)
        parts = (
            (slice(0, cols), jnp.dot(x, wq_own[at, :], preferred_element_type=F32)),
            (slice(cols, 2 * cols), jnp.dot(x, wq_other[at, :], preferred_element_type=F32)),
            (slice(2 * cols, acc.shape[1]), lax.dot_general(x, wkv, NT, preferred_element_type=F32)),
        )
        for where, part in parts:
            acc[:, where] = part if k == 0 else acc[:, where] + part

    cosine, sine = cos_ref[...], sin_ref[...]
    for head in range(2 * cols // HEAD_DIM):
        at = slice(head * HEAD_DIM, (head + 1) * HEAD_DIM)
        q_out[:, at] = turn(acc[:turned, at].astype(BF16), cosine, sine)
    raw = acc[:turned, 2 * cols :].astype(BF16)
    kv_out[:, :HEAD_DIM] = turn(raw[:, :HEAD_DIM], cosine, sine)
    kv_out[:, HEAD_DIM:] = raw[:, HEAD_DIM:]
    if dec_out is not None:
        dec_out[...] = acc[turned:, :].astype(BF16)


CUTS = (1, 2, 2, 2, 1)


def project(xs, pieces, turned, core, wq_own, wq_other, wkv_own, wkv_other, cosine, sine, name):
    total = sum(size for _, _, size in pieces)
    width = xs[0].shape[1]
    cols = wq_own.shape[1]
    wide = 2 * cols + 2 * HEAD_DIM
    cuts = [width * sum(CUTS[:k]) // sum(CUTS) for k in range(len(CUTS) + 1)]
    shapes = [(turned, 2 * cols), (turned, 2 * HEAD_DIM)]
    if total > turned:
        shapes.append((total - turned, wide))
    weights = (wq_own, wq_other, wkv_own, wkv_other)
    return pl.pallas_call(
        functools.partial(project_kernel, len(xs), pieces, cuts, turned),
        grid_spec=pltpu.PrefetchScalarGridSpec(
            num_scalar_prefetch=1,
            grid=(1,),
            in_specs=[pl.BlockSpec(memory_space=pl.ANY)] * (len(xs) + 4)
            + [pl.BlockSpec((turned, HEAD_DIM), lambda k, s: (0, 0))] * 2,
            out_specs=[pl.BlockSpec(shape, lambda k, s: (0, 0)) for shape in shapes],
            scratch_shapes=[pltpu.VMEM((total, wide), F32), pltpu.VMEM((total, width), BF16)]
            + [pltpu.VMEM(w.shape, BF16) for w in weights]
            + [pltpu.SemaphoreType.DMA((len(pieces) + 4, len(CUTS)))],
        ),
        out_shape=[jax.ShapeDtypeStruct(shape, BF16) for shape in shapes],
        compiler_params=pltpu.CompilerParams(vmem_limit_bytes=60 << 20),
        cost_estimate=pl.CostEstimate(
            flops=2 * total * width * wide, bytes_accessed=2 * width * (total + wide), transcendentals=0
        ),
        name=name,
    )(core, *xs, *weights, cosine, sine)


def attend_kernel(blocks, prefix, spec_ref, q_ref, pk_ref, pv_ref, *refs):
    own_refs, other_refs = refs[:2], refs[2:4]
    out_ref, k_all, v_all = refs[4:]
    first = jnp.logical_and(pl.program_id(0) == 0, pl.program_id(1) == 0)
    rows = out_ref.shape[0]

    @pl.when(first)
    def _():
        k_all[:prefix] = pk_ref[...]
        v_all[:prefix, :HEAD_DIM] = pv_ref[...]
        v_all[:, HEAD_DIM:] = jnp.ones((v_all.shape[0], HEAD_DIM), BF16)
        for j in range(2 * RING):
            place = spec_ref[1 + j]
            for refs_here, at in ((own_refs, place), (other_refs, place ^ 1)):
                block = refs_here[j // RING][(j % RING) * rows : (j % RING + 1) * rows, :]
                here = pl.ds(pl.multiple_of(prefix + at * rows, rows), rows)
                k_all[here, :] = block[:, :HEAD_DIM]
                v_all[here, :HEAD_DIM] = block[:, HEAD_DIM:]

    place = spec_ref[1 + 2 * RING + pl.program_id(0)]
    start = spec_ref[0]
    heads = q_ref.shape[1] // HEAD_DIM
    group = 4 * rows
    for level in range(RING):

        @pl.when(place // 4 == level)
        def _():
            keys = prefix + group * (level + 1)
            q = jnp.concatenate(
                [q_ref[:, h * HEAD_DIM : (h + 1) * HEAD_DIM] for h in range(heads)], axis=0
            )
            scores = lax.dot_general(q, k_all[:keys, :], NT, preferred_element_type=F32) * (
                HEAD_DIM**-0.5
            )
            half = prefix // 2
            last = keys - group
            col = lax.broadcasted_iota(jnp.int32, (heads * rows, half), 1) + half
            late = jnp.where(col < start, scores[:, half:prefix], -jnp.inf)
            row = lax.broadcasted_iota(jnp.int32, (heads * rows, group), 0) % rows
            own_col = lax.broadcasted_iota(jnp.int32, (heads * rows, group), 1)
            diag = jnp.where(
                own_col <= row + (place % 4) * rows, scores[:, last:], -jnp.inf
            )
            parts = [scores[:, :half], late]
            if last > prefix:
                parts.append(scores[:, prefix:last])
            parts.append(diag)
            top = functools.reduce(
                jnp.maximum, [jnp.max(p, axis=1, keepdims=True) for p in parts]
            )
            probs = jnp.concatenate([jnp.exp(p - top).astype(BF16) for p in parts], axis=1)
            mixed = jnp.dot(probs, v_all[:keys, :], preferred_element_type=F32)
            out = (mixed[:, :HEAD_DIM] / mixed[:, HEAD_DIM:]).astype(BF16)
            for h in range(heads):
                out_ref[:, h * HEAD_DIM : (h + 1) * HEAD_DIM] = out[h * rows : (h + 1) * rows]


def attend(spec, q, prefix_k, prefix_v, own, other, rows, name):
    prefix = prefix_k.shape[0]
    width = q.shape[1]
    blocks = RING
    total = prefix + 4 * RING * rows

    def whole(a):
        return pl.BlockSpec(a.shape, lambda i, g, s: (0, 0))

    return pl.pallas_call(
        functools.partial(attend_kernel, blocks, prefix),
        grid_spec=pltpu.PrefetchScalarGridSpec(
            num_scalar_prefetch=1,
            grid=(blocks, 2),
            in_specs=[
                pl.BlockSpec((rows, width // 2), lambda i, g, s: (i, g)),
                whole(prefix_k),
                whole(prefix_v),
            ]
            + [whole(a) for a in own + other],
            out_specs=pl.BlockSpec((rows, width // 2), lambda i, g, s: (i, g)),
            scratch_shapes=[
                pltpu.VMEM((total, HEAD_DIM), BF16),
                pltpu.VMEM((total, 2 * HEAD_DIM), BF16),
            ],
        ),
        out_shape=jax.ShapeDtypeStruct((blocks * rows, width), BF16),
        compiler_params=pltpu.CompilerParams(vmem_limit_bytes=60 << 20),
        cost_estimate=pl.CostEstimate(
            flops=4 * blocks * rows * width * total,
            bytes_accessed=2 * (2 * blocks * rows * width + 3 * total * HEAD_DIM),
            transcendentals=blocks * rows * width // HEAD_DIM * total,
        ),
        name=name,
    )(spec, q, prefix_k, prefix_v, *own, *other)


def emit_kernel(inputs, layout, *refs):
    xs, sources = refs[:inputs], refs[inputs : inputs + 2]
    outs, held, sems = refs[inputs + 2 : -3], refs[-3:-1], refs[-1]
    step = pl.program_id(0)
    half = held[0].shape[0]
    wide = outs[0].shape[1]

    def copies(k):
        at = pl.ds(pl.multiple_of(k * wide, wide), wide)
        for n in range(2):
            yield pltpu.make_async_copy(sources[n].at[:, at], held[n].at[:, at], sems.at[n, k])

    @pl.when(step == 0)
    def _():
        for k in range(sems.shape[1]):
            for copy in copies(k):
                copy.start()

    for copy in copies(step):
        copy.wait()
    here = pl.ds(pl.multiple_of(step * wide, wide), wide)
    x = jnp.concatenate([r[...] for r in xs], axis=0) if inputs > 1 else xs[0][...]
    partial = jnp.dot(x[:, :half], held[0][:, here], preferred_element_type=F32) + jnp.dot(
        x[:, half:], held[1][:, here], preferred_element_type=F32
    )
    partial = partial.astype(BF16)
    for out, spans in zip(outs, layout):
        at = 0
        for low, high in spans:
            out[at : at + high - low] = partial[low:high]
            at += high - low


def emit(xs, own, other, layout, name):
    sizes = [sum(high - low for low, high in spans) for spans in layout]
    total = sum(x.shape[0] for x in xs)
    half, width = own.shape
    wide = WIDE
    return pl.pallas_call(
        functools.partial(emit_kernel, len(xs), layout),
        grid=(width // wide,),
        in_specs=[pl.BlockSpec(x.shape, lambda n: (0, 0)) for x in xs]
        + [pl.BlockSpec(memory_space=pl.ANY)] * 2,
        out_specs=[pl.BlockSpec((size, wide), lambda n: (0, n)) for size in sizes],
        out_shape=[jax.ShapeDtypeStruct((size, width), BF16) for size in sizes],
        scratch_shapes=[pltpu.VMEM((half, width), BF16)] * 2
        + [pltpu.SemaphoreType.DMA((2, width // wide))],
        compiler_params=pltpu.CompilerParams(vmem_limit_bytes=60 << 20),
        cost_estimate=pl.CostEstimate(
            flops=4 * total * half * width,
            bytes_accessed=2 * (total * (2 * half + width) + 2 * half * width),
            transcendentals=0,
        ),
        name=name,
    )(*xs, own, other)


def frequencies():
    half_dim = HEAD_DIM // 2
    return jnp.exp(
        jnp.arange(half_dim, dtype=F32) * (-2.0 * math.log(500000.0) / HEAD_DIM)
    )


def tables(positions):
    angles = positions.astype(F32)[:, None] * frequencies()
    cosine, sine = jnp.cos(angles), jnp.sin(angles)
    return jnp.concatenate([cosine, cosine], 1), jnp.concatenate([-sine, sine], 1)


def rotate(values, positions):
    half_dim = values.shape[-1] // 2
    angles = positions[..., None] * frequencies()
    cosine, sine = jnp.cos(angles), jnp.sin(angles)
    widened = values.astype(F32)
    first, second = widened[..., :half_dim], widened[..., half_dim:]
    return jnp.concatenate(
        [first * cosine - second * sine, second * cosine + first * sine], -1
    ).astype(BF16)


def decode_attend(queries, new_keys, new_values, cached_keys, cached_values, lengths):
    rows, kv_heads, group_size, _ = queries.shape
    scale = HEAD_DIM**-0.5
    positions = lengths.astype(F32)
    q_rot = rotate(queries, positions[:, None, None])
    k_rot = rotate(new_keys, positions[:, None])
    span = cached_keys.shape[1]
    cache_k = cached_keys.reshape(rows, span, kv_heads, HEAD_DIM)
    cache_v = cached_values.reshape(rows, span, kv_heads, HEAD_DIM)
    old = jnp.einsum("rgjd,rlgd->rgjl", q_rot, cache_k, preferred_element_type=F32) * scale
    valid = jnp.arange(span, dtype=jnp.int32)[None, :] < lengths[:, None]
    old = jnp.where(valid[:, None, None, :], old, -jnp.inf)
    own = jnp.einsum("rgjd,rgd->rgj", q_rot, k_rot, preferred_element_type=F32) * scale
    top = jnp.maximum(jnp.max(old, axis=-1), own)
    old_weights = jnp.exp(old - top[..., None])
    own_weight = jnp.exp(own - top)
    total = jnp.sum(old_weights, axis=-1) + own_weight
    old_probs = (old_weights / total[..., None]).astype(BF16)
    own_prob = (own_weight / total).astype(BF16)
    mixed = jnp.einsum("rgjl,rlgd->rgjd", old_probs, cache_v, preferred_element_type=F32)
    mixed = mixed + own_prob.astype(F32)[..., None] * new_values.astype(F32)[:, :, None, :]
    return mixed.astype(BF16)


def add(*terms):
    return functools.reduce(lambda a, b: a + b, [t.astype(F32) for t in terms]).astype(BF16)


def shards(
    prefill_rows,
    decode_rows,
    norm_gain,
    w_query,
    w_key,
    w_value,
    w_out,
    prefix_keys,
    prefix_values,
    prefill_start,
    cache_keys,
    cache_values,
    cache_lengths,
):
    index = lax.axis_index("tensor")
    core, chip_x, chip_z = index & 1, (index >> 1) & 1, index >> 2
    rows = prefill_rows.shape[0]
    dec = decode_rows.shape[0]
    chips = 2 * RING
    half = rows // 2
    quarter = half // 2
    width = prefill_rows.shape[1]

    x0 = norm_rows(prefill_rows, norm_gain)
    dec_own = rms_norm(decode_rows, norm_gain)
    dec_rows = exchange(
        jnp.broadcast_to(dec_own[None], (chips, dec, width)).reshape(chips * dec, width)
    )
    wkv_own = jnp.concatenate([w_key.T, w_value.T], 0)
    pkv_own = jnp.concatenate([prefix_keys.T, prefix_values.T], 0)
    x1, x3, x2, wq_other, wkv_other = together(
        side(x0), up(x0), down(x0), swap(w_query), swap(wkv_own)
    )
    from_down, from_up, from_side, pkv_other = (
        up(jnp.concatenate([x1[:half], x3[:half]], 0)),
        down(jnp.concatenate([x1[:half], x2[half:]], 0)),
        side(jnp.concatenate([x2[half:], x3[half:]], 0)),
        swap(pkv_own),
    )
    wo_other = swap(w_out)

    low = jnp.where(core == 0, pkv_own, pkv_other)
    high = jnp.where(core == 0, pkv_other, pkv_own)
    kv_cols = prefix_keys.shape[1]
    prefix_k = jnp.concatenate([low[:kv_cols], high[:kv_cols]], 0).T
    prefix_v = jnp.concatenate([low[kv_cols:], high[kv_cols:]], 0).T

    places = []
    for z_off, flip in ((0, 0), (0, 1), (1, 0), (3, 0), (1, 1), (3, 1), (2, 0), (2, 1)):
        places.append((((chip_z + z_off) % RING) * 2 + (chip_x ^ flip)) * 2 + core)
    start = prefill_start[0]
    offsets = jnp.arange(rows, dtype=jnp.int32)
    near_pos = jnp.concatenate([start + p * rows + offsets for p in places[:4]])
    far_pos = jnp.concatenate([start + p * rows + offsets for p in places[4:]])
    near_cos, near_sin = tables(near_pos)
    far_cos, far_sin = tables(far_pos)
    core_spec = core.reshape(1).astype(jnp.int32)

    weights = (w_query, wq_other, wkv_own, wkv_other)
    turned = 4 * rows
    q_near, kv_near, dec_qkv = project(
        [x0, x1, x2, x3, dec_rows],
        [(i, 0, rows) for i in range(4)] + [(4, 0, chips * dec)],
        turned,
        core_spec,
        *weights,
        near_cos,
        near_sin,
        "project_near",
    )
    mine = exchange(dec_qkv)
    from_down, from_up, from_side, pkv_other, q_near, kv_near, mine = together(
        from_down, from_up, from_side, pkv_other, q_near, kv_near, mine
    )
    x7 = [up(from_down[:quarter]), down(from_up[quarter:half]), side(from_up[half:])]
    kv_near_other = swap(kv_near)
    q_cols = 2 * w_query.shape[1]
    mine = mine.reshape(chips, dec, -1).transpose(1, 0, 2)
    dec_attn = decode_attend(
        mine[:, :, :q_cols].reshape(dec, chips, q_cols // HEAD_DIM, HEAD_DIM),
        mine[:, :, q_cols : q_cols + HEAD_DIM],
        mine[:, :, q_cols + HEAD_DIM :],
        cache_keys,
        cache_values,
        cache_lengths,
    )
    dec_attn = exchange(
        dec_attn.reshape(dec, chips, q_cols).transpose(1, 0, 2).reshape(chips * dec, q_cols)
    )

    *x7, kv_near_other, dec_attn = together(*x7, kv_near_other, dec_attn)
    q_far, kv_far = project(
        [from_down, from_up, from_side, *x7],
        [(i, low, half) for i, low in ((1, 0), (2, 0), (0, 0), (2, half), (0, half), (1, half))]
        + [(3, 0, quarter), (4, 0, quarter), (5, 0, half)],
        turned,
        core_spec,
        *weights,
        far_cos,
        far_sin,
        "project_far",
    )
    kv_far_other = swap(kv_far)

    own, other = [kv_near, kv_far], [kv_near_other, kv_far_other]
    head = [start] + places
    far_spec = jnp.stack(head + places[4:]).astype(jnp.int32)
    near_spec = jnp.stack(head + places[:4]).astype(jnp.int32)
    attn_far = attend(far_spec, q_far, prefix_k, prefix_v, own, other, rows, "attend_far")

    def span(block, low, high):
        return (block * rows + low, block * rows + high)

    p_up, p_down, p_side, p7lo, p7hi, p7b = emit(
        [attn_far],
        w_out,
        wo_other,
        [
            [span(0, 0, half), span(2, half, rows)],
            [span(1, 0, half), span(2, 0, half)],
            [span(0, half, rows), span(1, half, rows)],
            [span(3, 0, quarter)],
            [span(3, quarter, half)],
            [span(3, half, rows)],
        ],
        "emit_far",
    )
    r6b, r4hi, r5lo, q_near = together(side(p7b), up(p7hi), down(p7lo), q_near)
    p_up = jnp.concatenate(
        [p_up[:quarter], add(p_up[quarter:half], r4hi), add(p_up[half:], r6b)], 0
    )
    p_down = jnp.concatenate([add(p_down[:quarter], r5lo), p_down[quarter:]], 0)
    r_up, r_down, r_side = up(p_up), down(p_down), side(p_side)
    attn_near = attend(near_spec, q_near, prefix_k, prefix_v, own, other, rows, "attend_near")
    p0, p1, p2, p3, pdec = emit(
        [attn_near, dec_attn],
        w_out,
        wo_other,
        [[span(i, 0, rows)] for i in range(4)] + [[(turned, turned + chips * dec)]],
        "emit_near",
    )
    r_up, r_down, r_side, p0, p1, p2, p3, pdec = together(
        r_up, r_down, r_side, p0, p1, p2, p3, pdec
    )
    p1 = jnp.concatenate([add(p1[:half], r_up[:half], r_down[:half]), p1[half:]], 0)
    p2 = jnp.concatenate([p2[:half], add(p2[half:], r_side[:half], r_up[half:])], 0)
    p3 = add(p3, jnp.concatenate([r_down[half:], r_side[half:]], 0))
    prefill_out = add(p0, *together(side(p1), up(p2), down(p3)))
    dec_parts = exchange(pdec).reshape(chips, dec, width)
    decode_out = jnp.sum(dec_parts.astype(F32), axis=0).astype(BF16)
    return (prefill_out, decode_out)


def solution(mesh):
    in_specs = (
        P(("dp", "tensor"), None),
        P(("dp", "tensor"), None),
        P(),
        P(None, "tensor"),
        P(None, "tensor"),
        P(None, "tensor"),
        P("tensor", None),
        P("dp", "tensor"),
        P("dp", "tensor"),
        P("dp"),
        P(("dp", "tensor"), None, None),
        P(("dp", "tensor"), None, None),
        P(("dp", "tensor")),
    )
    out_specs = (P(("dp", "tensor"), None), P(("dp", "tensor"), None))
    return jax.shard_map(shards, mesh=mesh, in_specs=in_specs, out_specs=out_specs, check_vma=False)
```

```python
import functools
import math

import jax
import jax.numpy as jnp
from jax import lax
from jax.experimental import pallas as pl
from jax.experimental.pallas import tpu as pltpu
from jax.sharding import PartitionSpec as P

HEAD_DIM = 128
RING = 4
BF16 = jnp.bfloat16
F32 = jnp.float32
NT = (((1,), (1,)), ((), ()))
WIDE = 2048
LIGHT = pl.CostEstimate(flops=1 << 20, bytes_accessed=1 << 16, transcendentals=0)


def route(move):
    pairs = []
    for z in range(RING):
        for x in range(2):
            for c in range(2):
                z2, x2, c2 = move(z, x, c)
                pairs.append(((z * 2 + x) * 2 + c, ((z2 % RING) * 2 + x2) * 2 + c2))
    return pairs


UP = route(lambda z, x, c: (z + 1, x, c))
DOWN = route(lambda z, x, c: (z - 1, x, c))
SIDE = route(lambda z, x, c: (z, 1 - x, c))
ACROSS = route(lambda z, x, c: (z + 2, x, c))
CORE = route(lambda z, x, c: (z, x, 1 - c))
SAME_CORE = [list(range(0, 4 * RING, 2)), list(range(1, 4 * RING, 2))]


def up(block):
    return lax.ppermute(block, "tensor", UP)


def down(block):
    return lax.ppermute(block, "tensor", DOWN)


def side(block):
    return lax.ppermute(block, "tensor", SIDE)


def across(block):
    return lax.ppermute(block, "tensor", ACROSS)


def swap(block):
    return lax.ppermute(block, "tensor", CORE)


def together(*arrays):
    return lax.optimization_barrier(arrays)


def exchange(block):
    return lax.all_to_all(
        block, "tensor", split_axis=0, concat_axis=0, axis_index_groups=SAME_CORE, tiled=True
    )


def norm_kernel(x_ref, gain_ref, out_ref, held, done, in_sems, out_sems):
    step = 16
    lanes = gain_ref.shape[1]
    count = held.shape[0] // step
    tiles = gain_ref.shape[0]
    ins = [
        pltpu.make_async_copy(
            x_ref.at[pl.ds(i * step, step), :], held.at[pl.ds(i * step, step), :], in_sems.at[i]
        )
        for i in range(count)
    ]
    outs = [
        pltpu.make_async_copy(
            done.at[pl.ds(i * step, step), :], out_ref.at[pl.ds(i * step, step), :], out_sems.at[i]
        )
        for i in range(count)
    ]
    for copy in ins:
        copy.start()
    gain = gain_ref[...].astype(F32)
    for i in range(count):
        ins[i].wait()
        at = slice(i * step, (i + 1) * step)
        total = jnp.zeros((step, lanes), F32)
        for t in range(tiles):
            widened = held[at, t * lanes : (t + 1) * lanes].astype(F32)
            total = total + widened * widened
        mean_sq = jnp.sum(total, axis=-1, keepdims=True) / (tiles * lanes)
        factor = jnp.broadcast_to(lax.rsqrt(mean_sq + 1e-05), (step, lanes))
        for t in range(tiles):
            here = slice(t * lanes, (t + 1) * lanes)
            widened = held[at, here].astype(F32)
            done[at, here] = (widened * factor * gain[t : t + 1, :]).astype(BF16)
        outs[i].start()
    for copy in outs:
        copy.wait()


def norm_rows(rows, gain):
    steps = rows.shape[0] // 16
    return pl.pallas_call(
        norm_kernel,
        in_specs=[
            pl.BlockSpec(memory_space=pl.ANY),
            pl.BlockSpec(gain.shape, lambda: (0, 0)),
        ],
        out_specs=pl.BlockSpec(memory_space=pl.ANY),
        out_shape=jax.ShapeDtypeStruct(rows.shape, BF16),
        scratch_shapes=[pltpu.VMEM(rows.shape, BF16)] * 2 + [pltpu.SemaphoreType.DMA((steps,))] * 2,
        compiler_params=pltpu.CompilerParams(vmem_limit_bytes=60 << 20),
        name="norm_rows",
    )(rows, gain)


def sum_kernel(inputs, outs_rows, terms, *refs):
    xs, outs = refs[:inputs], refs[inputs:]
    step = 16
    for out, rows, adds in zip(outs, outs_rows, terms):
        if len(adds) == 1 or all(at >= adds[k][2] + adds[k][3] for k, (_, _, at, _) in enumerate(adds[1:])):
            for i, first, at, size in adds:
                out[at : at + size] = xs[i][first : first + size]
            continue
        for low in range(0, rows, step):
            total = None
            for i, first, at, size in adds:
                if at <= low < at + size:
                    part = xs[i][first + low - at : first + low - at + step].astype(F32)
                    total = part if total is None else total + part
            out[low : low + step] = total.astype(BF16)


SPAN = 4096


def add_up(xs, outs_rows, terms, name):
    width = xs[0].shape[1]
    wide = SPAN
    return pl.pallas_call(
        functools.partial(sum_kernel, len(xs), outs_rows, terms),
        grid=(width // wide,),
        in_specs=[pl.BlockSpec((x.shape[0], wide), lambda n: (0, n)) for x in xs],
        out_specs=[pl.BlockSpec((rows, wide), lambda n: (0, n)) for rows in outs_rows],
        out_shape=[jax.ShapeDtypeStruct((rows, width), BF16) for rows in outs_rows],
        compiler_params=pltpu.CompilerParams(vmem_limit_bytes=60 << 20),
        cost_estimate=LIGHT,
        name=name,
    )(*xs)


def turn(values, cosine, signed_sine):
    widened = values.astype(F32)
    return (widened * cosine + pltpu.roll(widened, 64, 1) * signed_sine).astype(BF16)


def rms_norm(rows, gain):
    widened = rows.astype(F32)
    mean_sq = jnp.mean(widened * widened, axis=-1, keepdims=True)
    return (widened * lax.rsqrt(mean_sq + 1e-05) * gain.astype(F32)).astype(BF16)


def project_kernel(inputs, pieces, cuts, turned, core_ref, *refs):
    xs = refs[:inputs]
    sources, (cos_ref, sin_ref) = refs[inputs : inputs + 4], refs[inputs + 4 : inputs + 6]
    outs = refs[inputs + 6 :]
    q_out, kv_out = outs[:2]
    acc, rows, wq_own, wq_other, wkv_own, wkv_other, sems = outs[-7:]
    dec_out = outs[2] if len(outs) > 9 else None
    cols = wq_own.shape[1]

    def copies(k):
        at = pl.ds(cuts[k], cuts[k + 1] - cuts[k])
        low = 0
        for n, (i, first, size) in enumerate(pieces):
            yield pltpu.make_async_copy(
                xs[i].at[pl.ds(first, size), at], rows.at[pl.ds(low, size), at], sems.at[n, k]
            )
            low += size
        n = len(pieces)
        yield pltpu.make_async_copy(sources[0].at[at, :], wq_own.at[at, :], sems.at[n, k])
        yield pltpu.make_async_copy(sources[1].at[at, :], wq_other.at[at, :], sems.at[n + 1, k])
        yield pltpu.make_async_copy(sources[2].at[:, at], wkv_own.at[:, at], sems.at[n + 2, k])
        yield pltpu.make_async_copy(sources[3].at[:, at], wkv_other.at[:, at], sems.at[n + 3, k])

    steps = len(cuts) - 1
    for k in range(steps):
        for copy in copies(k):
            copy.start()
    own_low = core_ref[0] == 0
    for k in range(steps):
        at = slice(cuts[k], cuts[k + 1])
        for copy in copies(k):
            copy.wait()
        x = rows[:, at]
        own, other = wkv_own[:, at], wkv_other[:, at]
        low = jnp.where(own_low, own, other)
        high = jnp.where(own_low, other, own)
        wkv = jnp.concatenate([low[:64], high[:64], low[64:], high[64:]], axis=0)
        parts = (
            (slice(0, cols), jnp.dot(x, wq_own[at, :], preferred_element_type=F32)),
            (slice(cols, 2 * cols), jnp.dot(x, wq_other[at, :], preferred_element_type=F32)),
            (slice(2 * cols, acc.shape[1]), lax.dot_general(x, wkv, NT, preferred_element_type=F32)),
        )
        for where, part in parts:
            acc[:, where] = part if k == 0 else acc[:, where] + part

    cosine = jnp.concatenate([cos_ref[...], cos_ref[...]], axis=1)
    sine = jnp.concatenate([-sin_ref[...], sin_ref[...]], axis=1)
    for head in range(2 * cols // HEAD_DIM):
        at = slice(head * HEAD_DIM, (head + 1) * HEAD_DIM)
        q_out[:, at] = turn(acc[:turned, at].astype(BF16), cosine, sine)
    raw = acc[:turned, 2 * cols :].astype(BF16)
    kv_out[:, :HEAD_DIM] = turn(raw[:, :HEAD_DIM], cosine, sine)
    kv_out[:, HEAD_DIM:] = raw[:, HEAD_DIM:]
    if dec_out is not None:
        dec_out[...] = acc[turned:, :].astype(BF16)


CUTS = (1, 2, 2, 2, 1)


def project(xs, pieces, turned, core, weights, cosine, sine, part, name):
    total = sum(size for _, _, size in pieces)
    width = xs[0].shape[1]
    cols = weights[0].shape[1]
    wide = 2 * cols + 2 * HEAD_DIM
    cuts = [width * sum(CUTS[:k]) // sum(CUTS) for k in range(len(CUTS) + 1)]
    shapes = [(turned, 2 * cols), (turned, 2 * HEAD_DIM)]
    if total > turned:
        shapes.append((total - turned, wide))
    return pl.pallas_call(
        functools.partial(project_kernel, len(xs), pieces, cuts, turned),
        grid_spec=pltpu.PrefetchScalarGridSpec(
            num_scalar_prefetch=1,
            grid=(1,),
            in_specs=[pl.BlockSpec(memory_space=pl.ANY)] * (len(xs) + 4)
            + [pl.BlockSpec((turned, HEAD_DIM // 2), lambda k, s: (part, 0))] * 2,
            out_specs=[pl.BlockSpec(shape, lambda k, s: (0, 0)) for shape in shapes],
            scratch_shapes=[pltpu.VMEM((total, wide), F32), pltpu.VMEM((total, width), BF16)]
            + [pltpu.VMEM((width, cols), BF16)] * 2
            + [pltpu.VMEM((HEAD_DIM, width), BF16)] * 2
            + [pltpu.SemaphoreType.DMA((len(pieces) + 4, len(CUTS)))],
        ),
        out_shape=[jax.ShapeDtypeStruct(shape, BF16) for shape in shapes],
        compiler_params=pltpu.CompilerParams(vmem_limit_bytes=60 << 20),
        cost_estimate=LIGHT,
        name=name,
    )(core, *xs, *weights, cosine, sine)


def attend_kernel(prefix, blocks, layout, spec_ref, q_ref, own_pkv, other_pkv, *refs):
    own_refs, other_refs, sources = refs[:2], refs[2:4], refs[4:6]
    outs = refs[6:-6]
    k_all, v_all, late_bias, attn, held, sems = refs[-6:]
    rows = q_ref.shape[0]
    start = spec_ref[0]
    half = prefix // 2
    step = pl.program_id(0)
    wide = outs[0].shape[1]
    heads = q_ref.shape[1] // HEAD_DIM
    group = 4 * rows
    each = heads // CHAINS

    def copies(k):
        at = pl.ds(pl.multiple_of(k * wide, wide), wide)
        for n, source in enumerate(sources):
            deep = source.shape[0]
            to = held.at[pl.ds(n * deep, deep), at]
            yield pltpu.make_async_copy(source.at[:, at], to, sems.at[n, k])

    @pl.when(step == 0)
    def _():
        for k in range(sems.shape[1]):
            for copy in copies(k):
                copy.start()
        own_low = (spec_ref[1] & 1) == 0
        own, other = own_pkv[...], other_pkv[...]
        low = jnp.where(own_low, own, other)
        high = jnp.where(own_low, other, own)
        cols = HEAD_DIM // 2
        k_all[:prefix] = jnp.concatenate([low[:cols], high[:cols]], axis=0).T
        v_all[:prefix, :HEAD_DIM] = jnp.concatenate([low[cols:], high[cols:]], axis=0).T
        v_all[:, HEAD_DIM:] = jnp.ones((v_all.shape[0], HEAD_DIM), BF16)
        col = lax.broadcasted_iota(jnp.int32, late_bias.shape, 1) + half
        late_bias[...] = jnp.where(col < start, 0.0, -jnp.inf)
        for j in range(2 * RING):
            place = spec_ref[1 + j]
            for refs_here, at in ((own_refs, place), (other_refs, place ^ 1)):
                block = refs_here[j // RING][(j % RING) * rows : (j % RING + 1) * rows, :]
                here = pl.ds(pl.multiple_of(prefix + at * rows, rows), rows)
                k_all[here, :] = block[:, :HEAD_DIM]
                v_all[here, :HEAD_DIM] = block[:, HEAD_DIM:]

    place = spec_ref[1 + 2 * RING + jnp.minimum(step, blocks - 1)]
    here = pl.ds(pl.multiple_of(jnp.minimum(step, blocks - 1) * rows, rows), rows)
    for level in range(RING):

        @pl.when(jnp.logical_and(step < blocks, place // 4 == level))
        def _():
            keys = prefix + group * (level + 1)
            last = keys - group
            row = lax.broadcasted_iota(jnp.int32, (rows, group), 0)
            col = lax.broadcasted_iota(jnp.int32, (rows, group), 1)
            bias = jnp.where(col <= row + (place % 4) * rows, 0.0, -jnp.inf)
            bias = jnp.concatenate([bias] * each, axis=0)
            for chain in range(CHAINS):
                first = chain * each
                q = jnp.concatenate(
                    [q_ref[:, (first + h) * HEAD_DIM : (first + h + 1) * HEAD_DIM] for h in range(each)],
                    axis=0,
                )
                scores = lax.dot_general(q, k_all[:keys, :], NT, preferred_element_type=F32)
                parts = [scores[:, :half], scores[:, half:prefix] + late_bias[:1, :]]
                if last > prefix:
                    parts.append(scores[:, prefix:last])
                parts.append(scores[:, last:] + bias)
                slices = [
                    p[:, n : n + HEAD_DIM] for p in parts for n in range(0, p.shape[1], HEAD_DIM)
                ]
                top = jnp.max(functools.reduce(jnp.maximum, slices), axis=1, keepdims=True)
                scale = HEAD_DIM**-0.5
                probs = jnp.concatenate(
                    [jnp.exp((p - top) * scale).astype(BF16) for p in parts], axis=1
                )
                mixed = jnp.dot(probs, v_all[:keys, :], preferred_element_type=F32)
                out = (mixed[:, :HEAD_DIM] / mixed[:, HEAD_DIM:]).astype(BF16)
                for h in range(each):
                    at = slice((first + h) * HEAD_DIM, (first + h + 1) * HEAD_DIM)
                    attn[here, at] = out[h * rows : (h + 1) * rows]

    @pl.when(step >= blocks)
    def _():
        chunk = step - blocks
        for copy in copies(chunk):
            copy.wait()
        at = pl.ds(pl.multiple_of(chunk * wide, wide), wide)
        partial = jnp.dot(attn[...], held[:, at], preferred_element_type=F32).astype(BF16)
        for out, spans in zip(outs, layout):
            first = 0
            for low, high in spans:
                out[first : first + high - low] = partial[low:high]
                first += high - low


CHAINS = 4


def attend(spec, q, own_wide, other_wide, prefix, own, other, w_own, w_other, layout, rows, name):
    width = q.shape[1]
    blocks = q.shape[0] // rows
    total = prefix + 4 * RING * rows
    last = own_wide.shape[1] // prefix - 1
    deep, cols = w_own.shape
    wide = WIDE
    sizes = [sum(high - low for low, high in spans) for spans in layout]
    taken = sum(sizes)

    def whole(a):
        return pl.BlockSpec(a.shape, lambda i, s: (0, 0))

    return pl.pallas_call(
        functools.partial(attend_kernel, prefix, blocks, layout),
        grid_spec=pltpu.PrefetchScalarGridSpec(
            num_scalar_prefetch=1,
            grid=(blocks + cols // wide,),
            in_specs=[pl.BlockSpec((rows, width), lambda i, s: (jnp.minimum(i, blocks - 1), 0))]
            + [pl.BlockSpec((HEAD_DIM, prefix), lambda i, s: (0, last))] * 2
            + [whole(a) for a in own + other]
            + [pl.BlockSpec(memory_space=pl.ANY)] * 2,
            out_specs=[
                pl.BlockSpec((size, wide), lambda i, s: (0, jnp.maximum(i - blocks, 0)))
                for size in sizes
            ],
            scratch_shapes=[
                pltpu.VMEM((total, HEAD_DIM), BF16),
                pltpu.VMEM((total, 2 * HEAD_DIM), BF16),
                pltpu.VMEM((8, prefix // 2), F32),
                pltpu.VMEM((taken, width), BF16),
                pltpu.VMEM((2 * deep, cols), BF16),
                pltpu.SemaphoreType.DMA((2, cols // wide)),
            ],
        ),
        out_shape=[jax.ShapeDtypeStruct((size, cols), BF16) for size in sizes],
        compiler_params=pltpu.CompilerParams(vmem_limit_bytes=60 << 20),
        cost_estimate=LIGHT,
        name=name,
    )(spec, q, own_wide, other_wide, *own, *other, w_own, w_other)


def emit_kernel(inputs, layout, *refs):
    xs, sources = refs[:inputs], refs[inputs : inputs + 2]
    outs, held, sems = refs[inputs + 2 : -3], refs[-3:-1], refs[-1]
    step = pl.program_id(0)
    half = held[0].shape[0]
    wide = outs[0].shape[1]

    def copies(k):
        at = pl.ds(pl.multiple_of(k * wide, wide), wide)
        for n in range(2):
            yield pltpu.make_async_copy(sources[n].at[:, at], held[n].at[:, at], sems.at[n, k])

    @pl.when(step == 0)
    def _():
        for k in range(sems.shape[1]):
            for copy in copies(k):
                copy.start()

    for copy in copies(step):
        copy.wait()
    here = pl.ds(pl.multiple_of(step * wide, wide), wide)
    x = jnp.concatenate([r[...] for r in xs], axis=0) if inputs > 1 else xs[0][...]
    partial = jnp.dot(x[:, :half], held[0][:, here], preferred_element_type=F32) + jnp.dot(
        x[:, half:], held[1][:, here], preferred_element_type=F32
    )
    partial = partial.astype(BF16)
    for out, spans in zip(outs, layout):
        at = 0
        for low, high in spans:
            out[at : at + high - low] = partial[low:high]
            at += high - low


def emit(xs, own, other, layout, name):
    sizes = [sum(high - low for low, high in spans) for spans in layout]
    total = sum(x.shape[0] for x in xs)
    half, width = own.shape
    wide = WIDE
    return pl.pallas_call(
        functools.partial(emit_kernel, len(xs), layout),
        grid=(width // wide,),
        in_specs=[pl.BlockSpec(x.shape, lambda n: (0, 0)) for x in xs]
        + [pl.BlockSpec(memory_space=pl.ANY)] * 2,
        out_specs=[pl.BlockSpec((size, wide), lambda n: (0, n)) for size in sizes],
        out_shape=[jax.ShapeDtypeStruct((size, width), BF16) for size in sizes],
        scratch_shapes=[pltpu.VMEM((half, width), BF16)] * 2
        + [pltpu.SemaphoreType.DMA((2, width // wide))],
        compiler_params=pltpu.CompilerParams(vmem_limit_bytes=60 << 20),
        cost_estimate=LIGHT,
        name=name,
    )(*xs, own, other)


def frequencies():
    half_dim = HEAD_DIM // 2
    return jnp.exp(
        jnp.arange(half_dim, dtype=F32) * (-2.0 * math.log(500000.0) / HEAD_DIM)
    )


def rotate(values, positions):
    half_dim = values.shape[-1] // 2
    angles = positions[..., None] * frequencies()
    cosine, sine = jnp.cos(angles), jnp.sin(angles)
    widened = values.astype(F32)
    first, second = widened[..., :half_dim], widened[..., half_dim:]
    return jnp.concatenate(
        [first * cosine - second * sine, second * cosine + first * sine], -1
    ).astype(BF16)


def decode_attend(queries, new_keys, new_values, cached_keys, cached_values, lengths):
    rows, kv_heads, group_size, _ = queries.shape
    scale = HEAD_DIM**-0.5
    positions = lengths.astype(F32)
    q_rot = rotate(queries, positions[:, None, None])
    k_rot = rotate(new_keys, positions[:, None])
    span = cached_keys.shape[1]
    cache_k = cached_keys.reshape(rows, span, kv_heads, HEAD_DIM)
    cache_v = cached_values.reshape(rows, span, kv_heads, HEAD_DIM)
    old = jnp.einsum("rgjd,rlgd->rgjl", q_rot, cache_k, preferred_element_type=F32) * scale
    valid = jnp.arange(span, dtype=jnp.int32)[None, :] < lengths[:, None]
    old = jnp.where(valid[:, None, None, :], old, -jnp.inf)
    own = jnp.einsum("rgjd,rgd->rgj", q_rot, k_rot, preferred_element_type=F32) * scale
    top = jnp.maximum(jnp.max(old, axis=-1), own)
    old_weights = jnp.exp(old - top[..., None])
    own_weight = jnp.exp(own - top)
    total = jnp.sum(old_weights, axis=-1) + own_weight
    old_probs = (old_weights / total[..., None]).astype(BF16)
    own_prob = (own_weight / total).astype(BF16)
    mixed = jnp.einsum("rgjl,rlgd->rgjd", old_probs, cache_v, preferred_element_type=F32)
    mixed = mixed + own_prob.astype(F32)[..., None] * new_values.astype(F32)[:, :, None, :]
    return mixed.astype(BF16)


def shards(
    prefill_rows,
    decode_rows,
    norm_gain,
    w_query,
    w_key,
    w_value,
    w_out,
    prefix_keys,
    prefix_values,
    prefill_start,
    cache_keys,
    cache_values,
    cache_lengths,
):
    index = lax.axis_index("tensor")
    core, chip_x, chip_z = index & 1, (index >> 1) & 1, index >> 2
    rows = prefill_rows.shape[0]
    dec = decode_rows.shape[0]
    chips = 2 * RING
    half = rows // 2
    quarter = half // 2
    width = prefill_rows.shape[1]

    x0 = norm_rows(prefill_rows, norm_gain.reshape(width // 128, 128))
    x0, decode_rows, w_key, w_value = together(x0, decode_rows, w_key, w_value)
    dec_own = rms_norm(decode_rows, norm_gain)
    dec_rows = exchange(
        jnp.broadcast_to(dec_own[None], (chips, dec, width)).reshape(chips * dec, width)
    )
    kv_own = jnp.concatenate(
        [
            jnp.concatenate([w_key.T, w_value.T], 0),
            jnp.concatenate([prefix_keys.T, prefix_values.T], 0),
        ],
        1,
    )
    places = []
    for z_off, flip in ((0, 0), (0, 1), (1, 0), (3, 0), (1, 1), (3, 1), (2, 0), (2, 1)):
        places.append((((chip_z + z_off) % RING) * 2 + (chip_x ^ flip)) * 2 + core)
    start = prefill_start[0]
    spots = jnp.stack(places).astype(jnp.int32)
    positions = (start + spots[:, None] * rows + jnp.arange(rows, dtype=jnp.int32)[None]).reshape(-1)
    angles = positions.astype(F32)[:, None] * frequencies()
    cosine, sine = jnp.cos(angles), jnp.sin(angles)
    core_spec = core.reshape(1).astype(jnp.int32)
    head = jnp.concatenate([prefill_start, spots])
    near_spec = jnp.concatenate([head, spots[:RING]])
    far_spec = jnp.concatenate([head, spots[RING:]])

    x1, x3, x2, wq_other, kv_other, w_out, dec_rows, cosine, sine, near_spec, far_spec = together(
        side(x0),
        up(x0),
        down(x0),
        swap(w_query),
        swap(kv_own),
        w_out,
        dec_rows,
        cosine,
        sine,
        near_spec,
        far_spec,
    )
    x7 = across(x1)
    some = quarter
    rest = rows - some
    by_up, by_down, by_side = add_up(
        [x1, x2, x3],
        [some + half, some + half, 2 * rest],
        [
            [(0, 0, 0, some), (2, 0, some, half)],
            [(0, 0, 0, some), (1, half, some, half)],
            [(1, some, 0, rest), (2, some, rest, rest)],
        ],
        "regroup",
    )
    from_down, from_up, from_side = up(by_up), down(by_down), side(by_side)
    x1, x2, x3, *_ = together(x1, x2, x3, by_up, by_down, by_side)
    weights = (w_query, wq_other, kv_own, kv_other)
    turned = 4 * rows
    q_near, kv_near, dec_qkv = project(
        [x0, x1, x2, x3, dec_rows],
        [(i, 0, rows) for i in range(4)] + [(4, 0, chips * dec)],
        turned,
        core_spec,
        weights,
        cosine,
        sine,
        0,
        "project_near",
    )
    mine = exchange(dec_qkv)
    wo_other = swap(w_out)
    from_down, from_up, from_side, x7, mine, kv_near, wo_other = together(
        from_down, from_up, from_side, x7, mine, kv_near, wo_other
    )
    q_far, kv_far = project(
        [from_down, from_up, from_side, x7],
        [(1, 0, some), (2, 0, rest), (0, 0, some), (2, rest, rest), (0, some, half), (1, some, half)]
        + [(3, 0, rows)],
        turned,
        core_spec,
        weights,
        cosine,
        sine,
        1,
        "project_far",
    )
    kv_near, kv_far = together(kv_near, kv_far)
    kv_near_other, kv_far_other = swap(kv_near), swap(kv_far)

    own, other = [kv_near, kv_far], [kv_near_other, kv_far_other]
    prefix = prefix_keys.shape[0]
    def span(block, low, high):
        return (block * rows + low, block * rows + high)

    by_up, by_down, by_side, p7 = attend(
        far_spec,
        q_far,
        kv_own,
        kv_other,
        prefix,
        own,
        other,
        w_out,
        wo_other,
        [
            [span(0, 0, some), span(2, half, rows)],
            [span(1, 0, some), span(2, 0, half)],
            [span(0, some, rows), span(1, some, rows)],
            [span(3, 0, rows)],
        ],
        rows,
        "attend_far",
    )
    mine, q_near, by_up = together(mine, q_near, by_up)
    from_across, from_down, from_up, from_side = across(p7), up(by_up), down(by_down), side(by_side)
    q_cols = 2 * w_query.shape[1]
    mine = mine.reshape(chips, dec, -1).transpose(1, 0, 2)
    dec_attn = decode_attend(
        mine[:, :, :q_cols].reshape(dec, chips, q_cols // HEAD_DIM, HEAD_DIM),
        mine[:, :, q_cols : q_cols + HEAD_DIM],
        mine[:, :, q_cols + HEAD_DIM :],
        cache_keys,
        cache_values,
        cache_lengths,
    )
    dec_attn = exchange(
        dec_attn.reshape(dec, chips, q_cols).transpose(1, 0, 2).reshape(chips * dec, q_cols)
    )
    p0, p1, p2, p3 = attend(
        near_spec,
        q_near,
        kv_own,
        kv_other,
        prefix,
        own,
        other,
        w_out,
        wo_other,
        [[span(i, 0, rows)] for i in range(4)],
        rows,
        "attend_near",
    )
    p0, p1, p2, p3, from_down, from_up, from_side, from_across, dec_attn = together(
        p0, p1, p2, p3, from_down, from_up, from_side, from_across, dec_attn
    )
    p1, p2, p3 = add_up(
        [p1, p2, p3, from_down, from_up, from_side, from_across],
        [rows] * 3,
        [
            [(0, 0, 0, rows), (3, 0, 0, some), (4, 0, 0, some), (6, 0, 0, rows)],
            [(1, 0, 0, rows), (3, some, half, half), (5, 0, some, rest)],
            [(2, 0, 0, rows), (4, some, 0, half), (5, rest, some, rest)],
        ],
        "add_far",
    )
    (pdec,) = emit([dec_attn], w_out, wo_other, [[(0, chips * dec)]], "emit_decode")
    dec_parts = exchange(pdec).reshape(chips, dec, width)
    decode_out = jnp.sum(dec_parts.astype(F32), axis=0).astype(BF16)
    s1, s2, s3 = together(side(p1), up(p2), down(p3))
    (prefill_out,) = add_up(
        [p0, s1, s2, s3], [rows], [[(i, 0, 0, rows) for i in range(4)]], "add_near"
    )
    return (prefill_out, decode_out)


def solution(mesh):
    in_specs = (
        P(("dp", "tensor"), None),
        P(("dp", "tensor"), None),
        P(),
        P(None, "tensor"),
        P(None, "tensor"),
        P(None, "tensor"),
        P("tensor", None),
        P("dp", "tensor"),
        P("dp", "tensor"),
        P("dp"),
        P(("dp", "tensor"), None, None),
        P(("dp", "tensor"), None, None),
        P(("dp", "tensor")),
    )
    out_specs = (P(("dp", "tensor"), None), P(("dp", "tensor"), None))
    return jax.shard_map(shards, mesh=mesh, in_specs=in_specs, out_specs=out_specs, check_vma=False)
```

```python
import functools
import math

import jax
import jax.numpy as jnp
from jax import lax
from jax.experimental import pallas as pl
from jax.experimental.pallas import tpu as pltpu
from jax.sharding import PartitionSpec as P

HEAD_DIM = 128
RING = 4
BF16 = jnp.bfloat16
F32 = jnp.float32
NT = (((1,), (1,)), ((), ()))
WIDE = 2048
LIGHT = pl.CostEstimate(flops=1 << 20, bytes_accessed=1 << 16, transcendentals=0)


def route(move):
    pairs = []
    for z in range(RING):
        for x in range(2):
            for c in range(2):
                z2, x2, c2 = move(z, x, c)
                pairs.append(((z * 2 + x) * 2 + c, ((z2 % RING) * 2 + x2) * 2 + c2))
    return pairs


UP = route(lambda z, x, c: (z + 1, x, c))
DOWN = route(lambda z, x, c: (z - 1, x, c))
SIDE = route(lambda z, x, c: (z, 1 - x, c))
ACROSS = route(lambda z, x, c: (z + 2, x, c))
CORE = route(lambda z, x, c: (z, x, 1 - c))
SAME_CORE = [list(range(0, 4 * RING, 2)), list(range(1, 4 * RING, 2))]


def up(block):
    return lax.ppermute(block, "tensor", UP)


def down(block):
    return lax.ppermute(block, "tensor", DOWN)


def side(block):
    return lax.ppermute(block, "tensor", SIDE)


def across(block):
    return lax.ppermute(block, "tensor", ACROSS)


def swap(block):
    return lax.ppermute(block, "tensor", CORE)


def together(*arrays):
    return lax.optimization_barrier(arrays)


def exchange(block):
    return lax.all_to_all(
        block, "tensor", split_axis=0, concat_axis=0, axis_index_groups=SAME_CORE, tiled=True
    )


def norm_kernel(x_ref, gain_ref, out_ref, held, done, in_sems, out_sems):
    step = 16
    lanes = gain_ref.shape[1]
    count = held.shape[0] // step
    tiles = gain_ref.shape[0]
    ins = [
        pltpu.make_async_copy(
            x_ref.at[pl.ds(i * step, step), :], held.at[pl.ds(i * step, step), :], in_sems.at[i]
        )
        for i in range(count)
    ]
    outs = [
        pltpu.make_async_copy(
            done.at[pl.ds(i * step, step), :], out_ref.at[pl.ds(i * step, step), :], out_sems.at[i]
        )
        for i in range(count)
    ]
    for copy in ins:
        copy.start()
    gain = gain_ref[...].astype(F32)
    for i in range(count):
        ins[i].wait()
        at = slice(i * step, (i + 1) * step)
        total = jnp.zeros((step, lanes), F32)
        for t in range(tiles):
            widened = held[at, t * lanes : (t + 1) * lanes].astype(F32)
            total = total + widened * widened
        mean_sq = jnp.sum(total, axis=-1, keepdims=True) / (tiles * lanes)
        factor = jnp.broadcast_to(lax.rsqrt(mean_sq + 1e-05), (step, lanes))
        for t in range(tiles):
            here = slice(t * lanes, (t + 1) * lanes)
            widened = held[at, here].astype(F32)
            done[at, here] = (widened * factor * gain[t : t + 1, :]).astype(BF16)
        outs[i].start()
    for copy in outs:
        copy.wait()


def norm_rows(rows, gain):
    steps = rows.shape[0] // 16
    return pl.pallas_call(
        norm_kernel,
        in_specs=[
            pl.BlockSpec(memory_space=pl.ANY),
            pl.BlockSpec(gain.shape, lambda: (0, 0)),
        ],
        out_specs=pl.BlockSpec(memory_space=pl.ANY),
        out_shape=jax.ShapeDtypeStruct(rows.shape, BF16),
        scratch_shapes=[pltpu.VMEM(rows.shape, BF16)] * 2 + [pltpu.SemaphoreType.DMA((steps,))] * 2,
        compiler_params=pltpu.CompilerParams(vmem_limit_bytes=60 << 20),
        name="norm_rows",
    )(rows, gain)


def sum_kernel(inputs, outs_rows, terms, *refs):
    xs, outs = refs[:inputs], refs[inputs:]
    step = 16
    for out, rows, adds in zip(outs, outs_rows, terms):
        if len(adds) == 1 or all(at >= adds[k][2] + adds[k][3] for k, (_, _, at, _) in enumerate(adds[1:])):
            for i, first, at, size in adds:
                out[at : at + size] = xs[i][first : first + size]
            continue
        for low in range(0, rows, step):
            total = None
            for i, first, at, size in adds:
                if at <= low < at + size:
                    part = xs[i][first + low - at : first + low - at + step].astype(F32)
                    total = part if total is None else total + part
            out[low : low + step] = total.astype(BF16)


SPAN = 4096


def add_up(xs, outs_rows, terms, room, name):
    width = xs[0].shape[1]
    wide = SPAN
    return pl.pallas_call(
        functools.partial(sum_kernel, len(xs), outs_rows, terms),
        grid=(width // wide,),
        in_specs=[pl.BlockSpec((x.shape[0], wide), lambda n: (0, n)) for x in xs],
        out_specs=[pl.BlockSpec((rows, wide), lambda n: (0, n)) for rows in outs_rows],
        out_shape=[jax.ShapeDtypeStruct((rows, width), BF16) for rows in outs_rows],
        compiler_params=pltpu.CompilerParams(vmem_limit_bytes=room << 20),
        cost_estimate=LIGHT,
        name=name,
    )(*xs)


def turn(values, cosine, signed_sine):
    widened = values.astype(F32)
    return (widened * cosine + pltpu.roll(widened, 64, 1) * signed_sine).astype(BF16)


def rms_norm(rows, gain):
    widened = rows.astype(F32)
    mean_sq = jnp.mean(widened * widened, axis=-1, keepdims=True)
    return (widened * lax.rsqrt(mean_sq + 1e-05) * gain.astype(F32)).astype(BF16)


def project_kernel(inputs, pieces, cuts, turned, core_ref, *refs):
    xs = refs[:inputs]
    sources, (cos_ref, sin_ref) = refs[inputs : inputs + 4], refs[inputs + 4 : inputs + 6]
    outs = refs[inputs + 6 :]
    q_out, kv_out = outs[:2]
    acc, rows, wq_own, wq_other, wkv_own, wkv_other, sems = outs[-7:]
    dec_out = outs[2] if len(outs) > 9 else None
    cols = wq_own.shape[1]

    def copies(k):
        at = pl.ds(cuts[k], cuts[k + 1] - cuts[k])
        low = 0
        for n, (i, first, size) in enumerate(pieces):
            yield pltpu.make_async_copy(
                xs[i].at[pl.ds(first, size), at], rows.at[pl.ds(low, size), at], sems.at[n, k]
            )
            low += size
        n = len(pieces)
        yield pltpu.make_async_copy(sources[0].at[at, :], wq_own.at[at, :], sems.at[n, k])
        yield pltpu.make_async_copy(sources[1].at[at, :], wq_other.at[at, :], sems.at[n + 1, k])
        yield pltpu.make_async_copy(sources[2].at[:, at], wkv_own.at[:, at], sems.at[n + 2, k])
        yield pltpu.make_async_copy(sources[3].at[:, at], wkv_other.at[:, at], sems.at[n + 3, k])

    steps = len(cuts) - 1
    for k in range(steps):
        for copy in copies(k):
            copy.start()
    own_low = core_ref[0] == 0
    for k in range(steps):
        at = slice(cuts[k], cuts[k + 1])
        for copy in copies(k):
            copy.wait()
        x = rows[:, at]
        own, other = wkv_own[:, at], wkv_other[:, at]
        low = jnp.where(own_low, own, other)
        high = jnp.where(own_low, other, own)
        wkv = jnp.concatenate([low[:64], high[:64], low[64:], high[64:]], axis=0)
        parts = (
            (slice(0, cols), jnp.dot(x, wq_own[at, :], preferred_element_type=F32)),
            (slice(cols, 2 * cols), jnp.dot(x, wq_other[at, :], preferred_element_type=F32)),
            (slice(2 * cols, acc.shape[1]), lax.dot_general(x, wkv, NT, preferred_element_type=F32)),
        )
        for where, part in parts:
            acc[:, where] = part if k == 0 else acc[:, where] + part

    cosine = jnp.concatenate([cos_ref[...], cos_ref[...]], axis=1)
    sine = jnp.concatenate([-sin_ref[...], sin_ref[...]], axis=1)
    for head in range(2 * cols // HEAD_DIM):
        at = slice(head * HEAD_DIM, (head + 1) * HEAD_DIM)
        q_out[:, at] = turn(acc[:turned, at].astype(BF16), cosine, sine)
    raw = acc[:turned, 2 * cols :].astype(BF16)
    kv_out[:, :HEAD_DIM] = turn(raw[:, :HEAD_DIM], cosine, sine)
    kv_out[:, HEAD_DIM:] = raw[:, HEAD_DIM:]
    if dec_out is not None:
        dec_out[...] = acc[turned:, :].astype(BF16)


CUTS = (1, 2, 2, 2, 1)


def project(xs, pieces, turned, core, weights, cosine, sine, part, name):
    total = sum(size for _, _, size in pieces)
    width = xs[0].shape[1]
    cols = weights[0].shape[1]
    wide = 2 * cols + 2 * HEAD_DIM
    cuts = [width * sum(CUTS[:k]) // sum(CUTS) for k in range(len(CUTS) + 1)]
    shapes = [(turned, 2 * cols), (turned, 2 * HEAD_DIM)]
    if total > turned:
        shapes.append((total - turned, wide))
    return pl.pallas_call(
        functools.partial(project_kernel, len(xs), pieces, cuts, turned),
        grid_spec=pltpu.PrefetchScalarGridSpec(
            num_scalar_prefetch=1,
            grid=(1,),
            in_specs=[pl.BlockSpec(memory_space=pl.ANY)] * (len(xs) + 4)
            + [pl.BlockSpec((turned, HEAD_DIM // 2), lambda k, s: (part, 0))] * 2,
            out_specs=[pl.BlockSpec(shape, lambda k, s: (0, 0)) for shape in shapes],
            scratch_shapes=[pltpu.VMEM((total, wide), F32), pltpu.VMEM((total, width), BF16)]
            + [pltpu.VMEM((width, cols), BF16)] * 2
            + [pltpu.VMEM((HEAD_DIM, width), BF16)] * 2
            + [pltpu.SemaphoreType.DMA((len(pieces) + 4, len(CUTS)))],
        ),
        out_shape=[jax.ShapeDtypeStruct(shape, BF16) for shape in shapes],
        compiler_params=pltpu.CompilerParams(vmem_limit_bytes=60 << 20),
        cost_estimate=LIGHT,
        name=name,
    )(core, *xs, *weights, cosine, sine)


def attend_kernel(prefix, blocks, places, layout, extra, spec_ref, q_ref, own_pkv, other_pkv, *refs):
    own_refs, other_refs, (dec_ref, *sources) = refs[:2], refs[2:4], refs[4:7]
    terms, outs = refs[7 : 7 + len(extra)], refs[7 + len(extra) : -6]
    k_all, v_all, late_bias, attn, held, sems = refs[-6:]
    rows = q_ref.shape[0]
    start = spec_ref[0]
    half = prefix // 2
    step = pl.program_id(0)
    wide = outs[0].shape[1]
    heads = q_ref.shape[1] // HEAD_DIM
    group = 4 * rows
    each = heads // CHAINS

    def copies(k):
        at = pl.ds(pl.multiple_of(k * wide, wide), wide)
        for n, source in enumerate(sources):
            deep = source.shape[0]
            to = held.at[pl.ds(n * deep, deep), at]
            yield pltpu.make_async_copy(source.at[:, at], to, sems.at[n, k])

    @pl.when(step == 0)
    def _():
        for k in range(sems.shape[1]):
            for copy in copies(k):
                copy.start()
        if attn.shape[0] > blocks * rows:
            attn[blocks * rows :, :] = dec_ref[...]
        own_low = (spec_ref[1] & 1) == 0
        own, other = own_pkv[...], other_pkv[...]
        low = jnp.where(own_low, own, other)
        high = jnp.where(own_low, other, own)
        cols = HEAD_DIM // 2
        k_all[:prefix] = jnp.concatenate([low[:cols], high[:cols]], axis=0).T
        v_all[:prefix, :HEAD_DIM] = jnp.concatenate([low[cols:], high[cols:]], axis=0).T
        v_all[:, HEAD_DIM:] = jnp.ones((v_all.shape[0], HEAD_DIM), BF16)
        col = lax.broadcasted_iota(jnp.int32, late_bias.shape, 1) + half
        late_bias[...] = jnp.where(col < start, 0.0, -jnp.inf)
        for j in range(2 * RING):
            place = spec_ref[1 + j]
            for refs_here, at in ((own_refs, place), (other_refs, place ^ 1)):
                block = refs_here[j // RING][(j % RING) * rows : (j % RING + 1) * rows, :]
                here = pl.ds(pl.multiple_of(prefix + at * rows, rows), rows)
                k_all[here, :] = block[:, :HEAD_DIM]
                v_all[here, :HEAD_DIM] = block[:, HEAD_DIM:]

    place = spec_ref[1 + places[0] + places[1] * jnp.minimum(step, blocks - 1)]
    here = pl.ds(pl.multiple_of(jnp.minimum(step, blocks - 1) * rows, rows), rows)
    for level in range(RING):

        @pl.when(jnp.logical_and(step < blocks, place // 4 == level))
        def _():
            keys = prefix + group * (level + 1)
            last = keys - group
            row = lax.broadcasted_iota(jnp.int32, (rows, group), 0)
            col = lax.broadcasted_iota(jnp.int32, (rows, group), 1)
            bias = jnp.where(col <= row + (place % 4) * rows, 0.0, -jnp.inf)
            bias = jnp.concatenate([bias] * each, axis=0)
            for chain in range(CHAINS):
                first = chain * each
                q = jnp.concatenate(
                    [q_ref[:, (first + h) * HEAD_DIM : (first + h + 1) * HEAD_DIM] for h in range(each)],
                    axis=0,
                )
                scores = lax.dot_general(q, k_all[:keys, :], NT, preferred_element_type=F32)
                parts = [scores[:, :half], scores[:, half:prefix] + late_bias[:1, :]]
                if last > prefix:
                    parts.append(scores[:, prefix:last])
                parts.append(scores[:, last:] + bias)
                slices = [
                    p[:, n : n + HEAD_DIM] for p in parts for n in range(0, p.shape[1], HEAD_DIM)
                ]
                top = jnp.max(functools.reduce(jnp.maximum, slices), axis=1, keepdims=True)
                scale = HEAD_DIM**-0.5
                probs = jnp.concatenate(
                    [jnp.exp((p - top) * scale).astype(BF16) for p in parts], axis=1
                )
                mixed = jnp.dot(probs, v_all[:keys, :], preferred_element_type=F32)
                out = (mixed[:, :HEAD_DIM] / mixed[:, HEAD_DIM:]).astype(BF16)
                for h in range(each):
                    at = slice((first + h) * HEAD_DIM, (first + h + 1) * HEAD_DIM)
                    attn[here, at] = out[h * rows : (h + 1) * rows]

    @pl.when(step >= blocks)
    def _():
        chunk = step - blocks
        for copy in copies(chunk):
            copy.wait()
        at = pl.ds(pl.multiple_of(chunk * wide, wide), wide)
        partial = jnp.dot(attn[...], held[:, at], preferred_element_type=F32)
        for n, (out, (low, high)) in enumerate(zip(outs, layout)):
            total = partial[low:high]
            if n in extra:
                total = total.astype(BF16).astype(F32) + terms[extra.index(n)][...].astype(F32)
            out[...] = total.astype(BF16)


CHAINS = 4


def attend(spec, q, base, first, step, own_wide, other_wide, prefix, own, other, dec, w_own, w_other, layout, extra, terms, rows, name):
    width = q.shape[1]
    blocks = sum(high - low == rows for low, high in layout)
    total = prefix + 4 * RING * rows
    last = own_wide.shape[1] // prefix - 1
    deep, cols = w_own.shape
    wide = WIDE
    sizes = [high - low for low, high in layout]
    taken = sum(sizes)

    def whole(a):
        return pl.BlockSpec(a.shape, lambda i, s: (0, 0))

    return pl.pallas_call(
        functools.partial(attend_kernel, prefix, blocks, (base + first, step), layout, extra),
        grid_spec=pltpu.PrefetchScalarGridSpec(
            num_scalar_prefetch=1,
            grid=(blocks + cols // wide,),
            in_specs=[pl.BlockSpec((rows, width), lambda i, s: (first + step * jnp.minimum(i, blocks - 1), 0))]
            + [pl.BlockSpec((HEAD_DIM, prefix), lambda i, s: (0, last))] * 2
            + [whole(a) for a in own + other]
            + [pl.BlockSpec((max(taken - blocks * rows, 16), width), lambda i, s: (0, 0))]
            + [pl.BlockSpec(memory_space=pl.ANY)] * 2
            + [
                pl.BlockSpec((term.shape[0], wide), lambda i, s: (0, jnp.maximum(i - blocks, 0)))
                for term in terms
            ],
            out_specs=[
                pl.BlockSpec((size, wide), lambda i, s: (0, jnp.maximum(i - blocks, 0)))
                for size in sizes
            ],
            scratch_shapes=[
                pltpu.VMEM((total, HEAD_DIM), BF16),
                pltpu.VMEM((total, 2 * HEAD_DIM), BF16),
                pltpu.VMEM((8, prefix // 2), F32),
                pltpu.VMEM((taken, width), BF16),
                pltpu.VMEM((2 * deep, cols), BF16),
                pltpu.SemaphoreType.DMA((2, cols // wide)),
            ],
        ),
        out_shape=[jax.ShapeDtypeStruct((size, cols), BF16) for size in sizes],
        compiler_params=pltpu.CompilerParams(vmem_limit_bytes=60 << 20),
        cost_estimate=LIGHT,
        name=name,
    )(spec, q, own_wide, other_wide, *own, *other, q if dec is None else dec, w_own, w_other, *terms)


def frequencies():
    half_dim = HEAD_DIM // 2
    return jnp.exp(
        jnp.arange(half_dim, dtype=F32) * (-2.0 * math.log(500000.0) / HEAD_DIM)
    )


def rotate(values, positions):
    half_dim = values.shape[-1] // 2
    angles = positions[..., None] * frequencies()
    cosine, sine = jnp.cos(angles), jnp.sin(angles)
    widened = values.astype(F32)
    first, second = widened[..., :half_dim], widened[..., half_dim:]
    return jnp.concatenate(
        [first * cosine - second * sine, second * cosine + first * sine], -1
    ).astype(BF16)


def decode_attend(queries, new_keys, new_values, cached_keys, cached_values, lengths):
    rows, kv_heads, group_size, _ = queries.shape
    scale = HEAD_DIM**-0.5
    positions = lengths.astype(F32)
    q_rot = rotate(queries, positions[:, None, None])
    k_rot = rotate(new_keys, positions[:, None])
    span = cached_keys.shape[1]
    cache_k = cached_keys.reshape(rows, span, kv_heads, HEAD_DIM)
    cache_v = cached_values.reshape(rows, span, kv_heads, HEAD_DIM)
    old = jnp.einsum("rgjd,rlgd->rgjl", q_rot, cache_k, preferred_element_type=F32) * scale
    valid = jnp.arange(span, dtype=jnp.int32)[None, :] < lengths[:, None]
    old = jnp.where(valid[:, None, None, :], old, -jnp.inf)
    own = jnp.einsum("rgjd,rgd->rgj", q_rot, k_rot, preferred_element_type=F32) * scale
    top = jnp.maximum(jnp.max(old, axis=-1), own)
    old_weights = jnp.exp(old - top[..., None])
    own_weight = jnp.exp(own - top)
    total = jnp.sum(old_weights, axis=-1) + own_weight
    old_probs = (old_weights / total[..., None]).astype(BF16)
    own_prob = (own_weight / total).astype(BF16)
    mixed = jnp.einsum("rgjl,rlgd->rgjd", old_probs, cache_v, preferred_element_type=F32)
    mixed = mixed + own_prob.astype(F32)[..., None] * new_values.astype(F32)[:, :, None, :]
    return mixed.astype(BF16)


def shards(
    prefill_rows,
    decode_rows,
    norm_gain,
    w_query,
    w_key,
    w_value,
    w_out,
    prefix_keys,
    prefix_values,
    prefill_start,
    cache_keys,
    cache_values,
    cache_lengths,
):
    index = lax.axis_index("tensor")
    core, chip_x, chip_z = index & 1, (index >> 1) & 1, index >> 2
    rows = prefill_rows.shape[0]
    dec = decode_rows.shape[0]
    chips = 2 * RING
    half = rows // 2
    quarter = half // 2
    width = prefill_rows.shape[1]

    x0 = norm_rows(prefill_rows, norm_gain.reshape(width // 128, 128))
    x0, decode_rows, w_key, w_value = together(x0, decode_rows, w_key, w_value)
    dec_own = rms_norm(decode_rows, norm_gain)
    dec_rows = exchange(
        jnp.broadcast_to(dec_own[None], (chips, dec, width)).reshape(chips * dec, width)
    )
    kv_own = jnp.concatenate(
        [
            jnp.concatenate([w_key.T, w_value.T], 0),
            jnp.concatenate([prefix_keys.T, prefix_values.T], 0),
        ],
        1,
    )
    places = []
    for z_off, flip in ((0, 0), (0, 1), (1, 0), (3, 0), (1, 1), (3, 1), (2, 0), (2, 1)):
        places.append((((chip_z + z_off) % RING) * 2 + (chip_x ^ flip)) * 2 + core)
    start = prefill_start[0]
    spots = jnp.stack(places).astype(jnp.int32)
    positions = (start + spots[:, None] * rows + jnp.arange(rows, dtype=jnp.int32)[None]).reshape(-1)
    angles = positions.astype(F32)[:, None] * frequencies()
    cosine, sine = jnp.cos(angles), jnp.sin(angles)
    core_spec = core.reshape(1).astype(jnp.int32)
    spec = jnp.concatenate([prefill_start, spots])

    x1, x3, x2, wq_other, kv_other, w_out, dec_rows, cosine, sine, spec = together(
        side(x0),
        up(x0),
        down(x0),
        swap(w_query),
        swap(kv_own),
        w_out,
        dec_rows,
        cosine,
        sine,
        spec,
    )
    x7 = across(x1)
    some = quarter
    rest = rows - some
    by_up, by_down, by_side = add_up(
        [x1, x2, x3],
        [some + half, some + half, 2 * rest],
        [
            [(0, 0, 0, some), (2, 0, some, half)],
            [(0, 0, 0, some), (1, half, some, half)],
            [(1, some, 0, rest), (2, some, rest, rest)],
        ],
        24,
        "regroup",
    )
    from_down, from_up, from_side = up(by_up), down(by_down), side(by_side)
    x1, x2, x3, *_ = together(x1, x2, x3, by_up, by_down, by_side)
    weights = (w_query, wq_other, kv_own, kv_other)
    turned = 4 * rows
    q_near, kv_near, dec_qkv = project(
        [x0, x1, x2, x3, dec_rows],
        [(i, 0, rows) for i in range(4)] + [(4, 0, chips * dec)],
        turned,
        core_spec,
        weights,
        cosine,
        sine,
        0,
        "project_near",
    )
    mine = exchange(dec_qkv)
    wo_other = swap(w_out)
    from_down, from_up, from_side, x7, mine, kv_near, wo_other = together(
        from_down, from_up, from_side, x7, mine, kv_near, wo_other
    )
    q_far, kv_far = project(
        [from_down, from_up, from_side, x7],
        [(1, 0, some), (2, 0, rest), (0, 0, some), (2, rest, rest), (0, some, half), (1, some, half)]
        + [(3, 0, rows)],
        turned,
        core_spec,
        weights,
        cosine,
        sine,
        1,
        "project_far",
    )
    kv_near, kv_far = together(kv_near, kv_far)
    kv_near_other, kv_far_other = swap(kv_near), swap(kv_far)

    own, other = [kv_near, kv_far], [kv_near_other, kv_far_other]
    prefix = prefix_keys.shape[0]
    def cut(*sizes):
        ends = [sum(sizes[: i + 1]) for i in range(len(sizes))]
        return [(end - size, end) for size, end in zip(sizes, ends)]

    def attend_blocks(q, base, first, step, dec_attn, layout, extra, terms, name):
        return attend(
            spec,
            q,
            base,
            first,
            step,
            kv_own,
            kv_other,
            prefix,
            own,
            other,
            dec_attn,
            w_out,
            wo_other,
            layout,
            extra,
            terms,
            rows,
            name,
        )

    p4, p7 = attend_blocks(q_far, RING, 0, 3, None, cut(rows, rows), (), (), "attend_4_7")
    mine, q_far, p4, p7 = together(mine, q_far, p4, p7)
    r2, r1 = side(p4), across(p7)
    p5, p6 = attend_blocks(q_far, RING, 1, 1, None, cut(rows, rows), (), (), "attend_5_6")
    q_cols = 2 * w_query.shape[1]
    mine = mine.reshape(chips, dec, -1).transpose(1, 0, 2)
    dec_attn = decode_attend(
        mine[:, :, :q_cols].reshape(dec, chips, q_cols // HEAD_DIM, HEAD_DIM),
        mine[:, :, q_cols : q_cols + HEAD_DIM],
        mine[:, :, q_cols + HEAD_DIM :],
        cache_keys,
        cache_values,
        cache_lengths,
    )
    dec_attn = exchange(
        dec_attn.reshape(dec, chips, q_cols).transpose(1, 0, 2).reshape(chips * dec, q_cols)
    )
    q_near, p5, p6, r1, r2, dec_attn = together(q_near, p5, p6, r1, r2, dec_attn)
    r3_side, r3_down = side(p5), down(p6)
    p0, p1, p2, p3, pdec = attend_blocks(
        q_near,
        0,
        0,
        1,
        dec_attn,
        cut(*[rows] * 4, chips * dec),
        (1, 2),
        (r1, r2),
        "attend_near",
    )
    (p3,) = add_up([p3, r3_side, r3_down], [rows], [[(i, 0, 0, rows) for i in range(3)]], 60, "add_3")
    s1, s2, s3 = together(side(p1), up(p2), down(p3))
    dec_parts = exchange(pdec).reshape(chips, dec, width)
    decode_out = jnp.sum(dec_parts.astype(F32), axis=0).astype(BF16)
    (prefill_out,) = add_up(
        [p0, s1, s2, s3], [rows], [[(i, 0, 0, rows) for i in range(4)]], 24, "add_near"
    )
    return (prefill_out, decode_out)


def solution(mesh):
    in_specs = (
        P(("dp", "tensor"), None),
        P(("dp", "tensor"), None),
        P(),
        P(None, "tensor"),
        P(None, "tensor"),
        P(None, "tensor"),
        P("tensor", None),
        P("dp", "tensor"),
        P("dp", "tensor"),
        P("dp"),
        P(("dp", "tensor"), None, None),
        P(("dp", "tensor"), None, None),
        P(("dp", "tensor")),
    )
    out_specs = (P(("dp", "tensor"), None), P(("dp", "tensor"), None))
    return jax.shard_map(shards, mesh=mesh, in_specs=in_specs, out_specs=out_specs, check_vma=False)
```

```python
import functools
import math

import jax
import jax.numpy as jnp
from jax import lax
from jax.experimental import pallas as pl
from jax.experimental.pallas import tpu as pltpu
from jax.sharding import PartitionSpec as P

HEAD_DIM = 128
RING = 4
BF16 = jnp.bfloat16
F32 = jnp.float32
NT = (((1,), (1,)), ((), ()))
WIDE = 2048
LIGHT = pl.CostEstimate(flops=1 << 20, bytes_accessed=1 << 16, transcendentals=0)


def route(move):
    pairs = []
    for z in range(RING):
        for x in range(2):
            for c in range(2):
                z2, x2, c2 = move(z, x, c)
                pairs.append(((z * 2 + x) * 2 + c, ((z2 % RING) * 2 + x2) * 2 + c2))
    return pairs


UP = route(lambda z, x, c: (z + 1, x, c))
DOWN = route(lambda z, x, c: (z - 1, x, c))
SIDE = route(lambda z, x, c: (z, 1 - x, c))
ACROSS = route(lambda z, x, c: (z + 2, x, c))
CORE = route(lambda z, x, c: (z, x, 1 - c))
SAME_CORE = [list(range(0, 4 * RING, 2)), list(range(1, 4 * RING, 2))]


def up(block):
    return lax.ppermute(block, "tensor", UP)


def down(block):
    return lax.ppermute(block, "tensor", DOWN)


def side(block):
    return lax.ppermute(block, "tensor", SIDE)


def across(block):
    return lax.ppermute(block, "tensor", ACROSS)


def swap(block):
    return lax.ppermute(block, "tensor", CORE)


def together(*arrays):
    return lax.optimization_barrier(arrays)


def exchange(block):
    return lax.all_to_all(
        block, "tensor", split_axis=0, concat_axis=0, axis_index_groups=SAME_CORE, tiled=True
    )


def norm_kernel(x_ref, gain_ref, out_ref, held, done, in_sems, out_sems):
    step = 16
    lanes = gain_ref.shape[1]
    count = held.shape[0] // step
    tiles = gain_ref.shape[0]
    ins = [
        pltpu.make_async_copy(
            x_ref.at[pl.ds(i * step, step), :], held.at[pl.ds(i * step, step), :], in_sems.at[i]
        )
        for i in range(count)
    ]
    outs = [
        pltpu.make_async_copy(
            done.at[pl.ds(i * step, step), :], out_ref.at[pl.ds(i * step, step), :], out_sems.at[i]
        )
        for i in range(count)
    ]
    for copy in ins:
        copy.start()
    gain = gain_ref[...].astype(F32)
    for i in range(count):
        ins[i].wait()
        at = slice(i * step, (i + 1) * step)
        total = jnp.zeros((step, lanes), F32)
        for t in range(tiles):
            widened = held[at, t * lanes : (t + 1) * lanes].astype(F32)
            total = total + widened * widened
        mean_sq = jnp.sum(total, axis=-1, keepdims=True) / (tiles * lanes)
        factor = jnp.broadcast_to(lax.rsqrt(mean_sq + 1e-05), (step, lanes))
        for t in range(tiles):
            here = slice(t * lanes, (t + 1) * lanes)
            widened = held[at, here].astype(F32)
            done[at, here] = (widened * factor * gain[t : t + 1, :]).astype(BF16)
        outs[i].start()
    for copy in outs:
        copy.wait()


def norm_rows(rows, gain):
    steps = rows.shape[0] // 16
    return pl.pallas_call(
        norm_kernel,
        in_specs=[
            pl.BlockSpec(memory_space=pl.ANY),
            pl.BlockSpec(gain.shape, lambda: (0, 0)),
        ],
        out_specs=pl.BlockSpec(memory_space=pl.ANY),
        out_shape=jax.ShapeDtypeStruct(rows.shape, BF16),
        scratch_shapes=[pltpu.VMEM(rows.shape, BF16)] * 2 + [pltpu.SemaphoreType.DMA((steps,))] * 2,
        compiler_params=pltpu.CompilerParams(vmem_limit_bytes=60 << 20),
        name="norm_rows",
    )(rows, gain)


def sum_kernel(inputs, outs_rows, terms, *refs):
    xs, outs = refs[:inputs], refs[inputs:]
    step = 16
    for out, rows, adds in zip(outs, outs_rows, terms):
        if len(adds) == 1 or all(at >= adds[k][2] + adds[k][3] for k, (_, _, at, _) in enumerate(adds[1:])):
            for i, first, at, size in adds:
                out[at : at + size] = xs[i][first : first + size]
            continue
        for low in range(0, rows, step):
            total = None
            for i, first, at, size in adds:
                if at <= low < at + size:
                    part = xs[i][first + low - at : first + low - at + step].astype(F32)
                    total = part if total is None else total + part
            out[low : low + step] = total.astype(BF16)


SPAN = 4096


def add_up(xs, outs_rows, terms, room, name):
    width = xs[0].shape[1]
    wide = SPAN
    return pl.pallas_call(
        functools.partial(sum_kernel, len(xs), outs_rows, terms),
        grid=(width // wide,),
        in_specs=[pl.BlockSpec((x.shape[0], wide), lambda n: (0, n)) for x in xs],
        out_specs=[pl.BlockSpec((rows, wide), lambda n: (0, n)) for rows in outs_rows],
        out_shape=[jax.ShapeDtypeStruct((rows, width), BF16) for rows in outs_rows],
        compiler_params=pltpu.CompilerParams(vmem_limit_bytes=room << 20),
        cost_estimate=LIGHT,
        name=name,
    )(*xs)


def turn(values, cosine, signed_sine):
    widened = values.astype(F32)
    return (widened * cosine + pltpu.roll(widened, 64, 1) * signed_sine).astype(BF16)


def rms_norm(rows, gain):
    widened = rows.astype(F32)
    mean_sq = jnp.mean(widened * widened, axis=-1, keepdims=True)
    return (widened * lax.rsqrt(mean_sq + 1e-05) * gain.astype(F32)).astype(BF16)


def project_kernel(inputs, pieces, cuts, turned, core_ref, *refs):
    xs = refs[:inputs]
    sources, (cos_ref, sin_ref) = refs[inputs : inputs + 4], refs[inputs + 4 : inputs + 6]
    outs = refs[inputs + 6 :]
    q_out, kv_out = outs[:2]
    acc, rows, wq_own, wq_other, wkv_own, wkv_other, sems = outs[-7:]
    dec_out = outs[2] if len(outs) > 9 else None
    cols = wq_own.shape[1]

    def copies(k):
        at = pl.ds(cuts[k], cuts[k + 1] - cuts[k])
        low = 0
        for n, (i, first, size) in enumerate(pieces):
            yield pltpu.make_async_copy(
                xs[i].at[pl.ds(first, size), at], rows.at[pl.ds(low, size), at], sems.at[n, k]
            )
            low += size
        n = len(pieces)
        yield pltpu.make_async_copy(sources[0].at[at, :], wq_own.at[at, :], sems.at[n, k])
        yield pltpu.make_async_copy(sources[1].at[at, :], wq_other.at[at, :], sems.at[n + 1, k])
        yield pltpu.make_async_copy(sources[2].at[:, at], wkv_own.at[:, at], sems.at[n + 2, k])
        yield pltpu.make_async_copy(sources[3].at[:, at], wkv_other.at[:, at], sems.at[n + 3, k])

    steps = len(cuts) - 1
    for k in range(steps):
        for copy in copies(k):
            copy.start()
    own_low = core_ref[0] == 0
    for k in range(steps):
        at = slice(cuts[k], cuts[k + 1])
        for copy in copies(k):
            copy.wait()
        x = rows[:, at]
        own, other = wkv_own[:, at], wkv_other[:, at]
        low = jnp.where(own_low, own, other)
        high = jnp.where(own_low, other, own)
        wkv = jnp.concatenate([low[:64], high[:64], low[64:], high[64:]], axis=0)
        parts = (
            (slice(0, cols), jnp.dot(x, wq_own[at, :], preferred_element_type=F32)),
            (slice(cols, 2 * cols), jnp.dot(x, wq_other[at, :], preferred_element_type=F32)),
            (slice(2 * cols, acc.shape[1]), lax.dot_general(x, wkv, NT, preferred_element_type=F32)),
        )
        for where, part in parts:
            acc[:, where] = part if k == 0 else acc[:, where] + part

    cosine = jnp.concatenate([cos_ref[...], cos_ref[...]], axis=1)
    sine = jnp.concatenate([-sin_ref[...], sin_ref[...]], axis=1)
    for head in range(2 * cols // HEAD_DIM):
        at = slice(head * HEAD_DIM, (head + 1) * HEAD_DIM)
        q_out[:, at] = turn(acc[:turned, at].astype(BF16), cosine, sine)
    raw = acc[:turned, 2 * cols :].astype(BF16)
    kv_out[:, :HEAD_DIM] = turn(raw[:, :HEAD_DIM], cosine, sine)
    kv_out[:, HEAD_DIM:] = raw[:, HEAD_DIM:]
    if dec_out is not None:
        dec_out[...] = acc[turned:, :].astype(BF16)


CUTS = (1, 2, 2, 2, 1)


def project(xs, pieces, turned, core, weights, cosine, sine, part, name):
    total = sum(size for _, _, size in pieces)
    width = xs[0].shape[1]
    cols = weights[0].shape[1]
    wide = 2 * cols + 2 * HEAD_DIM
    cuts = [width * sum(CUTS[:k]) // sum(CUTS) for k in range(len(CUTS) + 1)]
    shapes = [(turned, 2 * cols), (turned, 2 * HEAD_DIM)]
    if total > turned:
        shapes.append((total - turned, wide))
    return pl.pallas_call(
        functools.partial(project_kernel, len(xs), pieces, cuts, turned),
        grid_spec=pltpu.PrefetchScalarGridSpec(
            num_scalar_prefetch=1,
            grid=(1,),
            in_specs=[pl.BlockSpec(memory_space=pl.ANY)] * (len(xs) + 4)
            + [pl.BlockSpec((turned, HEAD_DIM // 2), lambda k, s: (part, 0))] * 2,
            out_specs=[pl.BlockSpec(shape, lambda k, s: (0, 0)) for shape in shapes],
            scratch_shapes=[pltpu.VMEM((total, wide), F32), pltpu.VMEM((total, width), BF16)]
            + [pltpu.VMEM((width, cols), BF16)] * 2
            + [pltpu.VMEM((HEAD_DIM, width), BF16)] * 2
            + [pltpu.SemaphoreType.DMA((len(pieces) + 4, len(CUTS)))],
        ),
        out_shape=[jax.ShapeDtypeStruct(shape, BF16) for shape in shapes],
        compiler_params=pltpu.CompilerParams(vmem_limit_bytes=60 << 20),
        cost_estimate=LIGHT,
        name=name,
    )(core, *xs, *weights, cosine, sine)


def attend_kernel(prefix, blocks, places, layout, extra, spec_ref, q_ref, own_pkv, other_pkv, *refs):
    own_refs, other_refs, (dec_ref, *sources) = refs[:2], refs[2:4], refs[4:7]
    terms, outs = refs[7 : 7 + len(extra)], refs[7 + len(extra) : -6]
    k_all, v_all, late_bias, attn, held, sems = refs[-6:]
    rows = q_ref.shape[0]
    start = spec_ref[0]
    half = prefix // 2
    step = pl.program_id(0)
    wide = outs[0].shape[1]
    heads = q_ref.shape[1] // HEAD_DIM
    group = 4 * rows
    each = heads // CHAINS

    def copies(k):
        at = pl.ds(pl.multiple_of(k * wide, wide), wide)
        for n, source in enumerate(sources):
            deep = source.shape[0]
            to = held.at[pl.ds(n * deep, deep), at]
            yield pltpu.make_async_copy(source.at[:, at], to, sems.at[n, k])

    @pl.when(step == 0)
    def _():
        for k in range(sems.shape[1]):
            for copy in copies(k):
                copy.start()
        if attn.shape[0] > blocks * rows:
            attn[blocks * rows :, :] = dec_ref[...]
        own_low = (spec_ref[1] & 1) == 0
        own, other = own_pkv[...], other_pkv[...]
        low = jnp.where(own_low, own, other)
        high = jnp.where(own_low, other, own)
        cols = HEAD_DIM // 2
        k_all[:prefix] = jnp.concatenate([low[:cols], high[:cols]], axis=0).T
        v_all[:prefix, :HEAD_DIM] = jnp.concatenate([low[cols:], high[cols:]], axis=0).T
        v_all[:, HEAD_DIM:] = jnp.ones((v_all.shape[0], HEAD_DIM), BF16)
        col = lax.broadcasted_iota(jnp.int32, late_bias.shape, 1) + half
        late_bias[...] = jnp.where(col < start, 0.0, -jnp.inf)
        for j in range(2 * RING):
            place = spec_ref[1 + j]
            for refs_here, at in ((own_refs, place), (other_refs, place ^ 1)):
                block = refs_here[j // RING][(j % RING) * rows : (j % RING + 1) * rows, :]
                here = pl.ds(pl.multiple_of(prefix + at * rows, rows), rows)
                k_all[here, :] = block[:, :HEAD_DIM]
                v_all[here, :HEAD_DIM] = block[:, HEAD_DIM:]

    place = spec_ref[1 + places[0] + places[1] * jnp.minimum(step, blocks - 1)]
    here = pl.ds(pl.multiple_of(jnp.minimum(step, blocks - 1) * rows, rows), rows)
    for level in range(RING):

        @pl.when(jnp.logical_and(step < blocks, place // 4 == level))
        def _():
            keys = prefix + group * (level + 1)
            last = keys - group
            row = lax.broadcasted_iota(jnp.int32, (rows, group), 0)
            col = lax.broadcasted_iota(jnp.int32, (rows, group), 1)
            bias = jnp.where(col <= row + (place % 4) * rows, 0.0, -jnp.inf)
            bias = jnp.concatenate([bias] * each, axis=0)
            for chain in range(CHAINS):
                first = chain * each
                q = jnp.concatenate(
                    [q_ref[:, (first + h) * HEAD_DIM : (first + h + 1) * HEAD_DIM] for h in range(each)],
                    axis=0,
                )
                scores = lax.dot_general(q, k_all[:keys, :], NT, preferred_element_type=F32)
                parts = [scores[:, :half], scores[:, half:prefix] + late_bias[:1, :]]
                if last > prefix:
                    parts.append(scores[:, prefix:last])
                parts.append(scores[:, last:] + bias)
                slices = [
                    p[:, n : n + HEAD_DIM] for p in parts for n in range(0, p.shape[1], HEAD_DIM)
                ]
                top = jnp.max(functools.reduce(jnp.maximum, slices), axis=1, keepdims=True)
                scale = HEAD_DIM**-0.5
                probs = jnp.concatenate(
                    [jnp.exp((p - top) * scale).astype(BF16) for p in parts], axis=1
                )
                mixed = jnp.dot(probs, v_all[:keys, :], preferred_element_type=F32)
                out = (mixed[:, :HEAD_DIM] / mixed[:, HEAD_DIM:]).astype(BF16)
                for h in range(each):
                    at = slice((first + h) * HEAD_DIM, (first + h + 1) * HEAD_DIM)
                    attn[here, at] = out[h * rows : (h + 1) * rows]

    @pl.when(step >= blocks)
    def _():
        chunk = step - blocks
        for copy in copies(chunk):
            copy.wait()
        at = pl.ds(pl.multiple_of(chunk * wide, wide), wide)
        partial = jnp.dot(attn[...], held[:, at], preferred_element_type=F32)
        for n, (out, (low, high)) in enumerate(zip(outs, layout)):
            total = partial[low:high]
            if n in extra:
                total = total.astype(BF16).astype(F32) + terms[extra.index(n)][...].astype(F32)
            out[...] = total.astype(BF16)


CHAINS = 4


def attend(spec, q, base, first, step, own_wide, other_wide, prefix, own, other, dec, w_own, w_other, layout, extra, terms, rows, name):
    width = q.shape[1]
    blocks = sum(high - low == rows for low, high in layout)
    total = prefix + 4 * RING * rows
    last = own_wide.shape[1] // prefix - 1
    deep, cols = w_own.shape
    wide = WIDE
    sizes = [high - low for low, high in layout]
    taken = sum(sizes)

    def whole(a):
        return pl.BlockSpec(a.shape, lambda i, s: (0, 0))

    return pl.pallas_call(
        functools.partial(attend_kernel, prefix, blocks, (base + first, step), layout, extra),
        grid_spec=pltpu.PrefetchScalarGridSpec(
            num_scalar_prefetch=1,
            grid=(blocks + cols // wide,),
            in_specs=[pl.BlockSpec((rows, width), lambda i, s: (first + step * jnp.minimum(i, blocks - 1), 0))]
            + [pl.BlockSpec((HEAD_DIM, prefix), lambda i, s: (0, last))] * 2
            + [whole(a) for a in own + other]
            + [pl.BlockSpec((max(taken - blocks * rows, 16), width), lambda i, s: (0, 0))]
            + [pl.BlockSpec(memory_space=pl.ANY)] * 2
            + [
                pl.BlockSpec((term.shape[0], wide), lambda i, s: (0, jnp.maximum(i - blocks, 0)))
                for term in terms
            ],
            out_specs=[
                pl.BlockSpec((size, wide), lambda i, s: (0, jnp.maximum(i - blocks, 0)))
                for size in sizes
            ],
            scratch_shapes=[
                pltpu.VMEM((total, HEAD_DIM), BF16),
                pltpu.VMEM((total, 2 * HEAD_DIM), BF16),
                pltpu.VMEM((8, prefix // 2), F32),
                pltpu.VMEM((taken, width), BF16),
                pltpu.VMEM((2 * deep, cols), BF16),
                pltpu.SemaphoreType.DMA((2, cols // wide)),
            ],
        ),
        out_shape=[jax.ShapeDtypeStruct((size, cols), BF16) for size in sizes],
        compiler_params=pltpu.CompilerParams(vmem_limit_bytes=56 << 20),
        cost_estimate=LIGHT,
        name=name,
    )(spec, q, own_wide, other_wide, *own, *other, q if dec is None else dec, w_own, w_other, *terms)


def frequencies():
    half_dim = HEAD_DIM // 2
    return jnp.exp(
        jnp.arange(half_dim, dtype=F32) * (-2.0 * math.log(500000.0) / HEAD_DIM)
    )


def rotate(values, positions):
    half_dim = values.shape[-1] // 2
    angles = positions[..., None] * frequencies()
    cosine, sine = jnp.cos(angles), jnp.sin(angles)
    widened = values.astype(F32)
    first, second = widened[..., :half_dim], widened[..., half_dim:]
    return jnp.concatenate(
        [first * cosine - second * sine, second * cosine + first * sine], -1
    ).astype(BF16)


def decode_attend(queries, new_keys, new_values, cached_keys, cached_values, lengths):
    rows, kv_heads, group_size, _ = queries.shape
    scale = HEAD_DIM**-0.5
    positions = lengths.astype(F32)
    q_rot = rotate(queries, positions[:, None, None])
    k_rot = rotate(new_keys, positions[:, None])
    span = cached_keys.shape[1]
    cache_k = cached_keys.reshape(rows, span, kv_heads, HEAD_DIM)
    cache_v = cached_values.reshape(rows, span, kv_heads, HEAD_DIM)
    old = jnp.einsum("rgjd,rlgd->rgjl", q_rot, cache_k, preferred_element_type=F32) * scale
    valid = jnp.arange(span, dtype=jnp.int32)[None, :] < lengths[:, None]
    old = jnp.where(valid[:, None, None, :], old, -jnp.inf)
    own = jnp.einsum("rgjd,rgd->rgj", q_rot, k_rot, preferred_element_type=F32) * scale
    top = jnp.maximum(jnp.max(old, axis=-1), own)
    old_weights = jnp.exp(old - top[..., None])
    own_weight = jnp.exp(own - top)
    total = jnp.sum(old_weights, axis=-1) + own_weight
    old_probs = (old_weights / total[..., None]).astype(BF16)
    own_prob = (own_weight / total).astype(BF16)
    mixed = jnp.einsum("rgjl,rlgd->rgjd", old_probs, cache_v, preferred_element_type=F32)
    mixed = mixed + own_prob.astype(F32)[..., None] * new_values.astype(F32)[:, :, None, :]
    return mixed.astype(BF16)


def shards(
    prefill_rows,
    decode_rows,
    norm_gain,
    w_query,
    w_key,
    w_value,
    w_out,
    prefix_keys,
    prefix_values,
    prefill_start,
    cache_keys,
    cache_values,
    cache_lengths,
):
    index = lax.axis_index("tensor")
    core, chip_x, chip_z = index & 1, (index >> 1) & 1, index >> 2
    rows = prefill_rows.shape[0]
    dec = decode_rows.shape[0]
    chips = 2 * RING
    half = rows // 2
    quarter = half // 2
    width = prefill_rows.shape[1]

    x0 = norm_rows(prefill_rows, norm_gain.reshape(width // 128, 128))
    x0, decode_rows, w_key, w_value = together(x0, decode_rows, w_key, w_value)
    dec_own = rms_norm(decode_rows, norm_gain)
    dec_rows = exchange(
        jnp.broadcast_to(dec_own[None], (chips, dec, width)).reshape(chips * dec, width)
    )
    kv_own = jnp.concatenate(
        [
            jnp.concatenate([w_key.T, w_value.T], 0),
            jnp.concatenate([prefix_keys.T, prefix_values.T], 0),
        ],
        1,
    )
    places = []
    for z_off, flip in ((0, 0), (0, 1), (1, 0), (3, 0), (1, 1), (3, 1), (2, 0), (2, 1)):
        places.append((((chip_z + z_off) % RING) * 2 + (chip_x ^ flip)) * 2 + core)
    start = prefill_start[0]
    spots = jnp.stack(places).astype(jnp.int32)
    positions = (start + spots[:, None] * rows + jnp.arange(rows, dtype=jnp.int32)[None]).reshape(-1)
    angles = positions.astype(F32)[:, None] * frequencies()
    cosine, sine = jnp.cos(angles), jnp.sin(angles)
    core_spec = core.reshape(1).astype(jnp.int32)
    spec = jnp.concatenate([prefill_start, spots])

    x1, x3, x2, wq_other, kv_other, w_out, dec_rows, cosine, sine, spec = together(
        side(x0),
        up(x0),
        down(x0),
        swap(w_query),
        swap(kv_own),
        w_out,
        dec_rows,
        cosine,
        sine,
        spec,
    )
    x7 = across(x1)
    some = quarter
    rest = rows - some
    by_up, by_down, by_side = add_up(
        [x1, x2, x3],
        [some + half, some + half, 2 * rest],
        [
            [(0, 0, 0, some), (2, 0, some, half)],
            [(0, 0, 0, some), (1, half, some, half)],
            [(1, some, 0, rest), (2, some, rest, rest)],
        ],
        24,
        "regroup",
    )
    from_down, from_up, from_side = up(by_up), down(by_down), side(by_side)
    x1, x2, x3, *_ = together(x1, x2, x3, by_up, by_down, by_side)
    weights = (w_query, wq_other, kv_own, kv_other)
    turned = 4 * rows
    q_near, kv_near, dec_qkv = project(
        [x0, x1, x2, x3, dec_rows],
        [(i, 0, rows) for i in range(4)] + [(4, 0, chips * dec)],
        turned,
        core_spec,
        weights,
        cosine,
        sine,
        0,
        "project_near",
    )
    mine = exchange(dec_qkv)
    wo_other = swap(w_out)
    from_down, from_up, from_side, x7, mine, kv_near, wo_other = together(
        from_down, from_up, from_side, x7, mine, kv_near, wo_other
    )
    q_far, kv_far = project(
        [from_down, from_up, from_side, x7],
        [(1, 0, some), (2, 0, rest), (0, 0, some), (2, rest, rest), (0, some, half), (1, some, half)]
        + [(3, 0, rows)],
        turned,
        core_spec,
        weights,
        cosine,
        sine,
        1,
        "project_far",
    )
    kv_near, kv_far = together(kv_near, kv_far)
    kv_near_other, kv_far_other = swap(kv_near), swap(kv_far)

    own, other = [kv_near, kv_far], [kv_near_other, kv_far_other]
    prefix = prefix_keys.shape[0]
    def cut(*sizes):
        ends = [sum(sizes[: i + 1]) for i in range(len(sizes))]
        return [(end - size, end) for size, end in zip(sizes, ends)]

    def attend_blocks(q, base, first, step, dec_attn, layout, extra, terms, name):
        return attend(
            spec,
            q,
            base,
            first,
            step,
            kv_own,
            kv_other,
            prefix,
            own,
            other,
            dec_attn,
            w_out,
            wo_other,
            layout,
            extra,
            terms,
            rows,
            name,
        )

    p4, p7 = attend_blocks(q_far, RING, 0, 3, None, cut(rows, rows), (), (), "attend_4_7")
    mine, q_far, p4, p7 = together(mine, q_far, p4, p7)
    r2, r1 = side(p4), across(p7)
    p5, p6 = attend_blocks(q_far, RING, 1, 1, None, cut(rows, rows), (), (), "attend_5_6")
    q_cols = 2 * w_query.shape[1]
    mine = mine.reshape(chips, dec, -1).transpose(1, 0, 2)
    dec_attn = decode_attend(
        mine[:, :, :q_cols].reshape(dec, chips, q_cols // HEAD_DIM, HEAD_DIM),
        mine[:, :, q_cols : q_cols + HEAD_DIM],
        mine[:, :, q_cols + HEAD_DIM :],
        cache_keys,
        cache_values,
        cache_lengths,
    )
    dec_attn = exchange(
        dec_attn.reshape(dec, chips, q_cols).transpose(1, 0, 2).reshape(chips * dec, q_cols)
    )
    q_near, p5, p6, r1, r2, dec_attn = together(q_near, p5, p6, r1, r2, dec_attn)
    r3_side, r3_down = side(p5), down(p6)
    p0, p1, p2, p3, pdec = attend_blocks(
        q_near,
        0,
        0,
        1,
        dec_attn,
        cut(*[rows] * 4, chips * dec),
        (1, 2),
        (r1, r2),
        "attend_near",
    )
    (p3,) = add_up([p3, r3_side, r3_down], [rows], [[(i, 0, 0, rows) for i in range(3)]], 56, "add_3")
    s1, s2, s3 = together(side(p1), up(p2), down(p3))
    dec_parts = exchange(pdec).reshape(chips, dec, width)
    decode_out = jnp.sum(dec_parts.astype(F32), axis=0).astype(BF16)
    (prefill_out,) = add_up(
        [p0, s1, s2, s3], [rows], [[(i, 0, 0, rows) for i in range(4)]], 24, "add_near"
    )
    return (prefill_out, decode_out)


def solution(mesh):
    in_specs = (
        P(("dp", "tensor"), None),
        P(("dp", "tensor"), None),
        P(),
        P(None, "tensor"),
        P(None, "tensor"),
        P(None, "tensor"),
        P("tensor", None),
        P("dp", "tensor"),
        P("dp", "tensor"),
        P("dp"),
        P(("dp", "tensor"), None, None),
        P(("dp", "tensor"), None, None),
        P(("dp", "tensor")),
    )
    out_specs = (P(("dp", "tensor"), None), P(("dp", "tensor"), None))
    return jax.shard_map(shards, mesh=mesh, in_specs=in_specs, out_specs=out_specs, check_vma=False)
```

```python
import functools
import math

import jax
import jax.numpy as jnp
from jax import lax
from jax.experimental import pallas as pl
from jax.experimental.pallas import tpu as pltpu
from jax.sharding import PartitionSpec as P

HEAD_DIM = 128
RING = 4
BF16 = jnp.bfloat16
F32 = jnp.float32
NT = (((1,), (1,)), ((), ()))
WIDE = 2048
LIGHT = pl.CostEstimate(flops=1 << 20, bytes_accessed=1 << 16, transcendentals=0)


def route(move):
    pairs = []
    for z in range(RING):
        for x in range(2):
            for c in range(2):
                z2, x2, c2 = move(z, x, c)
                pairs.append(((z * 2 + x) * 2 + c, ((z2 % RING) * 2 + x2) * 2 + c2))
    return pairs


UP = route(lambda z, x, c: (z + 1, x, c))
DOWN = route(lambda z, x, c: (z - 1, x, c))
SIDE = route(lambda z, x, c: (z, 1 - x, c))
ACROSS = route(lambda z, x, c: (z + 2, x, c))
CORE = route(lambda z, x, c: (z, x, 1 - c))
SAME_CORE = [list(range(0, 4 * RING, 2)), list(range(1, 4 * RING, 2))]


def up(block):
    return lax.ppermute(block, "tensor", UP)


def down(block):
    return lax.ppermute(block, "tensor", DOWN)


def side(block):
    return lax.ppermute(block, "tensor", SIDE)


def across(block):
    return lax.ppermute(block, "tensor", ACROSS)


def swap(block):
    return lax.ppermute(block, "tensor", CORE)


def together(*arrays):
    return lax.optimization_barrier(arrays)


def exchange(block):
    return lax.all_to_all(
        block, "tensor", split_axis=0, concat_axis=0, axis_index_groups=SAME_CORE, tiled=True
    )


def norm_kernel(x_ref, gain_ref, out_ref, held, done, in_sems, out_sems):
    step = 16
    lanes = gain_ref.shape[1]
    count = held.shape[0] // step
    tiles = gain_ref.shape[0]
    ins = [
        pltpu.make_async_copy(
            x_ref.at[pl.ds(i * step, step), :], held.at[pl.ds(i * step, step), :], in_sems.at[i]
        )
        for i in range(count)
    ]
    outs = [
        pltpu.make_async_copy(
            done.at[pl.ds(i * step, step), :], out_ref.at[pl.ds(i * step, step), :], out_sems.at[i]
        )
        for i in range(count)
    ]
    for copy in ins:
        copy.start()
    gain = gain_ref[...].astype(F32)
    for i in range(count):
        ins[i].wait()
        at = slice(i * step, (i + 1) * step)
        total = jnp.zeros((step, lanes), F32)
        for t in range(tiles):
            widened = held[at, t * lanes : (t + 1) * lanes].astype(F32)
            total = total + widened * widened
        mean_sq = jnp.sum(total, axis=-1, keepdims=True) / (tiles * lanes)
        factor = jnp.broadcast_to(lax.rsqrt(mean_sq + 1e-05), (step, lanes))
        for t in range(tiles):
            here = slice(t * lanes, (t + 1) * lanes)
            widened = held[at, here].astype(F32)
            done[at, here] = (widened * factor * gain[t : t + 1, :]).astype(BF16)
        outs[i].start()
    for copy in outs:
        copy.wait()


def norm_rows(rows, gain):
    steps = rows.shape[0] // 16
    return pl.pallas_call(
        norm_kernel,
        in_specs=[
            pl.BlockSpec(memory_space=pl.ANY),
            pl.BlockSpec(gain.shape, lambda: (0, 0)),
        ],
        out_specs=pl.BlockSpec(memory_space=pl.ANY),
        out_shape=jax.ShapeDtypeStruct(rows.shape, BF16),
        scratch_shapes=[pltpu.VMEM(rows.shape, BF16)] * 2 + [pltpu.SemaphoreType.DMA((steps,))] * 2,
        compiler_params=pltpu.CompilerParams(vmem_limit_bytes=60 << 20),
        name="norm_rows",
    )(rows, gain)


def sum_kernel(inputs, outs_rows, terms, *refs):
    xs, outs = refs[:inputs], refs[inputs:]
    step = 16
    for out, rows, adds in zip(outs, outs_rows, terms):
        if len(adds) == 1 or all(at >= adds[k][2] + adds[k][3] for k, (_, _, at, _) in enumerate(adds[1:])):
            for i, first, at, size in adds:
                out[at : at + size] = xs[i][first : first + size]
            continue
        for low in range(0, rows, step):
            total = None
            for i, first, at, size in adds:
                if at <= low < at + size:
                    part = xs[i][first + low - at : first + low - at + step].astype(F32)
                    total = part if total is None else total + part
            out[low : low + step] = total.astype(BF16)


SPAN = 4096


def add_up(xs, outs_rows, terms, room, name):
    width = xs[0].shape[1]
    wide = SPAN
    return pl.pallas_call(
        functools.partial(sum_kernel, len(xs), outs_rows, terms),
        grid=(width // wide,),
        in_specs=[pl.BlockSpec((x.shape[0], wide), lambda n: (0, n)) for x in xs],
        out_specs=[pl.BlockSpec((rows, wide), lambda n: (0, n)) for rows in outs_rows],
        out_shape=[jax.ShapeDtypeStruct((rows, width), BF16) for rows in outs_rows],
        compiler_params=pltpu.CompilerParams(vmem_limit_bytes=room << 20),
        cost_estimate=LIGHT,
        name=name,
    )(*xs)


def turn(values, cosine, signed_sine):
    widened = values.astype(F32)
    return (widened * cosine + pltpu.roll(widened, 64, 1) * signed_sine).astype(BF16)


def rms_norm(rows, gain):
    widened = rows.astype(F32)
    mean_sq = jnp.mean(widened * widened, axis=-1, keepdims=True)
    return (widened * lax.rsqrt(mean_sq + 1e-05) * gain.astype(F32)).astype(BF16)


def project_kernel(inputs, pieces, cuts, turned, core_ref, *refs):
    xs = refs[:inputs]
    sources, (cos_ref, sin_ref) = refs[inputs : inputs + 4], refs[inputs + 4 : inputs + 6]
    outs = refs[inputs + 6 :]
    q_out, kv_out = outs[:2]
    acc, rows, wq_own, wq_other, wkv_own, wkv_other, sems = outs[-7:]
    dec_out = outs[2] if len(outs) > 9 else None
    cols = wq_own.shape[1]

    def copies(k):
        at = pl.ds(cuts[k], cuts[k + 1] - cuts[k])
        low = 0
        for n, (i, first, size) in enumerate(pieces):
            yield pltpu.make_async_copy(
                xs[i].at[pl.ds(first, size), at], rows.at[pl.ds(low, size), at], sems.at[n, k]
            )
            low += size
        n = len(pieces)
        yield pltpu.make_async_copy(sources[0].at[at, :], wq_own.at[at, :], sems.at[n, k])
        yield pltpu.make_async_copy(sources[1].at[at, :], wq_other.at[at, :], sems.at[n + 1, k])
        yield pltpu.make_async_copy(sources[2].at[:, at], wkv_own.at[:, at], sems.at[n + 2, k])
        yield pltpu.make_async_copy(sources[3].at[:, at], wkv_other.at[:, at], sems.at[n + 3, k])

    steps = len(cuts) - 1
    for k in range(steps):
        for copy in copies(k):
            copy.start()
    own_low = core_ref[0] == 0
    for k in range(steps):
        at = slice(cuts[k], cuts[k + 1])
        for copy in copies(k):
            copy.wait()
        x = rows[:, at]
        own, other = wkv_own[:, at], wkv_other[:, at]
        low = jnp.where(own_low, own, other)
        high = jnp.where(own_low, other, own)
        wkv = jnp.concatenate([low[:64], high[:64], low[64:], high[64:]], axis=0)
        parts = (
            (slice(0, cols), jnp.dot(x, wq_own[at, :], preferred_element_type=F32)),
            (slice(cols, 2 * cols), jnp.dot(x, wq_other[at, :], preferred_element_type=F32)),
            (slice(2 * cols, acc.shape[1]), lax.dot_general(x, wkv, NT, preferred_element_type=F32)),
        )
        for where, part in parts:
            acc[:, where] = part if k == 0 else acc[:, where] + part

    cosine = jnp.concatenate([cos_ref[...], cos_ref[...]], axis=1)
    sine = jnp.concatenate([-sin_ref[...], sin_ref[...]], axis=1)
    for head in range(2 * cols // HEAD_DIM):
        at = slice(head * HEAD_DIM, (head + 1) * HEAD_DIM)
        q_out[:, at] = turn(acc[:turned, at].astype(BF16), cosine, sine)
    raw = acc[:turned, 2 * cols :].astype(BF16)
    kv_out[:, :HEAD_DIM] = turn(raw[:, :HEAD_DIM], cosine, sine)
    kv_out[:, HEAD_DIM:] = raw[:, HEAD_DIM:]
    if dec_out is not None:
        dec_out[...] = acc[turned:, :].astype(BF16)


CUTS = (1, 2, 2, 2, 1)


def project(xs, pieces, turned, core, weights, cosine, sine, part, name):
    total = sum(size for _, _, size in pieces)
    width = xs[0].shape[1]
    cols = weights[0].shape[1]
    wide = 2 * cols + 2 * HEAD_DIM
    cuts = [width * sum(CUTS[:k]) // sum(CUTS) for k in range(len(CUTS) + 1)]
    shapes = [(turned, 2 * cols), (turned, 2 * HEAD_DIM)]
    if total > turned:
        shapes.append((total - turned, wide))
    return pl.pallas_call(
        functools.partial(project_kernel, len(xs), pieces, cuts, turned),
        grid_spec=pltpu.PrefetchScalarGridSpec(
            num_scalar_prefetch=1,
            grid=(1,),
            in_specs=[pl.BlockSpec(memory_space=pl.ANY)] * (len(xs) + 4)
            + [pl.BlockSpec((turned, HEAD_DIM // 2), lambda k, s: (part, 0))] * 2,
            out_specs=[pl.BlockSpec(shape, lambda k, s: (0, 0)) for shape in shapes],
            scratch_shapes=[pltpu.VMEM((total, wide), F32), pltpu.VMEM((total, width), BF16)]
            + [pltpu.VMEM((width, cols), BF16)] * 2
            + [pltpu.VMEM((HEAD_DIM, width), BF16)] * 2
            + [pltpu.SemaphoreType.DMA((len(pieces) + 4, len(CUTS)))],
        ),
        out_shape=[jax.ShapeDtypeStruct(shape, BF16) for shape in shapes],
        compiler_params=pltpu.CompilerParams(vmem_limit_bytes=60 << 20),
        cost_estimate=LIGHT,
        name=name,
    )(core, *xs, *weights, cosine, sine)


def attend_kernel(prefix, blocks, places, layout, extra, spec_ref, q_ref, own_pkv, other_pkv, *refs):
    own_refs, other_refs, (dec_ref, *sources) = refs[:2], refs[2:4], refs[4:7]
    terms, outs = refs[7 : 7 + len(extra)], refs[7 + len(extra) : -6]
    k_all, v_all, late_bias, attn, held, sems = refs[-6:]
    rows = q_ref.shape[0]
    start = spec_ref[0]
    half = prefix // 2
    step = pl.program_id(0)
    wide = outs[0].shape[1]
    heads = q_ref.shape[1] // HEAD_DIM
    group = 4 * rows
    each = heads // CHAINS

    def copies(k):
        at = pl.ds(pl.multiple_of(k * wide, wide), wide)
        for n, source in enumerate(sources):
            deep = source.shape[0]
            to = held.at[pl.ds(n * deep, deep), at]
            yield pltpu.make_async_copy(source.at[:, at], to, sems.at[n, k])

    @pl.when(step == 0)
    def _():
        for k in range(sems.shape[1]):
            for copy in copies(k):
                copy.start()
        if attn.shape[0] > blocks * rows:
            attn[blocks * rows :, :] = dec_ref[...]
        own_low = (spec_ref[1] & 1) == 0
        own, other = own_pkv[...], other_pkv[...]
        low = jnp.where(own_low, own, other)
        high = jnp.where(own_low, other, own)
        cols = HEAD_DIM // 2
        k_all[:prefix] = jnp.concatenate([low[:cols], high[:cols]], axis=0).T
        v_all[:prefix, :HEAD_DIM] = jnp.concatenate([low[cols:], high[cols:]], axis=0).T
        v_all[:, HEAD_DIM:] = jnp.ones((v_all.shape[0], HEAD_DIM), BF16)
        col = lax.broadcasted_iota(jnp.int32, late_bias.shape, 1) + half
        late_bias[...] = jnp.where(col < start, 0.0, -jnp.inf)
        for j in range(2 * RING):
            place = spec_ref[1 + j]
            for refs_here, at in ((own_refs, place), (other_refs, place ^ 1)):
                block = refs_here[j // RING][(j % RING) * rows : (j % RING + 1) * rows, :]
                here = pl.ds(pl.multiple_of(prefix + at * rows, rows), rows)
                k_all[here, :] = block[:, :HEAD_DIM]
                v_all[here, :HEAD_DIM] = block[:, HEAD_DIM:]

    place = spec_ref[1 + places[0] + places[1] * jnp.minimum(step, blocks - 1)]
    here = pl.ds(pl.multiple_of(jnp.minimum(step, blocks - 1) * rows, rows), rows)
    for level in range(RING):

        @pl.when(jnp.logical_and(step < blocks, place // 4 == level))
        def _():
            keys = prefix + group * (level + 1)
            last = keys - group
            row = lax.broadcasted_iota(jnp.int32, (rows, group), 0)
            col = lax.broadcasted_iota(jnp.int32, (rows, group), 1)
            bias = jnp.where(col <= row + (place % 4) * rows, 0.0, -jnp.inf)
            bias = jnp.concatenate([bias] * each, axis=0)
            for chain in range(CHAINS):
                first = chain * each
                q = jnp.concatenate(
                    [q_ref[:, (first + h) * HEAD_DIM : (first + h + 1) * HEAD_DIM] for h in range(each)],
                    axis=0,
                )
                scores = lax.dot_general(q, k_all[:keys, :], NT, preferred_element_type=F32)
                parts = [scores[:, :half], scores[:, half:prefix] + late_bias[:1, :]]
                if last > prefix:
                    parts.append(scores[:, prefix:last])
                parts.append(scores[:, last:] + bias)
                slices = [
                    p[:, n : n + HEAD_DIM] for p in parts for n in range(0, p.shape[1], HEAD_DIM)
                ]
                top = jnp.max(functools.reduce(jnp.maximum, slices), axis=1, keepdims=True)
                scale = HEAD_DIM**-0.5 * math.log2(math.e)
                probs = jnp.concatenate(
                    [jnp.exp2((p - top) * scale).astype(BF16) for p in parts], axis=1
                )
                mixed = jnp.dot(probs, v_all[:keys, :], preferred_element_type=F32)
                out = (mixed[:, :HEAD_DIM] / mixed[:, HEAD_DIM:]).astype(BF16)
                for h in range(each):
                    at = slice((first + h) * HEAD_DIM, (first + h + 1) * HEAD_DIM)
                    attn[here, at] = out[h * rows : (h + 1) * rows]

    @pl.when(step >= blocks)
    def _():
        chunk = step - blocks
        for copy in copies(chunk):
            copy.wait()
        at = pl.ds(pl.multiple_of(chunk * wide, wide), wide)
        partial = jnp.dot(attn[...], held[:, at], preferred_element_type=F32)
        for n, (out, (low, high)) in enumerate(zip(outs, layout)):
            total = partial[low:high]
            if n in extra:
                total = total.astype(BF16).astype(F32) + terms[extra.index(n)][...].astype(F32)
            out[...] = total.astype(BF16)


CHAINS = 4


def attend(spec, q, base, first, step, own_wide, other_wide, prefix, own, other, dec, w_own, w_other, layout, extra, terms, rows, name):
    width = q.shape[1]
    blocks = sum(high - low == rows for low, high in layout)
    total = prefix + 4 * RING * rows
    last = own_wide.shape[1] // prefix - 1
    deep, cols = w_own.shape
    wide = WIDE
    sizes = [high - low for low, high in layout]
    taken = sum(sizes)

    def whole(a):
        return pl.BlockSpec(a.shape, lambda i, s: (0, 0))

    return pl.pallas_call(
        functools.partial(attend_kernel, prefix, blocks, (base + first, step), layout, extra),
        grid_spec=pltpu.PrefetchScalarGridSpec(
            num_scalar_prefetch=1,
            grid=(blocks + cols // wide,),
            in_specs=[pl.BlockSpec((rows, width), lambda i, s: (first + step * jnp.minimum(i, blocks - 1), 0))]
            + [pl.BlockSpec((HEAD_DIM, prefix), lambda i, s: (0, last))] * 2
            + [whole(a) for a in own + other]
            + [pl.BlockSpec((max(taken - blocks * rows, 16), width), lambda i, s: (0, 0))]
            + [pl.BlockSpec(memory_space=pl.ANY)] * 2
            + [
                pl.BlockSpec((term.shape[0], wide), lambda i, s: (0, jnp.maximum(i - blocks, 0)))
                for term in terms
            ],
            out_specs=[
                pl.BlockSpec((size, wide), lambda i, s: (0, jnp.maximum(i - blocks, 0)))
                for size in sizes
            ],
            scratch_shapes=[
                pltpu.VMEM((total, HEAD_DIM), BF16),
                pltpu.VMEM((total, 2 * HEAD_DIM), BF16),
                pltpu.VMEM((8, prefix // 2), F32),
                pltpu.VMEM((taken, width), BF16),
                pltpu.VMEM((2 * deep, cols), BF16),
                pltpu.SemaphoreType.DMA((2, cols // wide)),
            ],
        ),
        out_shape=[jax.ShapeDtypeStruct((size, cols), BF16) for size in sizes],
        compiler_params=pltpu.CompilerParams(vmem_limit_bytes=56 << 20),
        cost_estimate=LIGHT,
        name=name,
    )(spec, q, own_wide, other_wide, *own, *other, q if dec is None else dec, w_own, w_other, *terms)


def frequencies():
    half_dim = HEAD_DIM // 2
    return jnp.exp(
        jnp.arange(half_dim, dtype=F32) * (-2.0 * math.log(500000.0) / HEAD_DIM)
    )


def rotate(values, positions):
    half_dim = values.shape[-1] // 2
    angles = positions[..., None] * frequencies()
    cosine, sine = jnp.cos(angles), jnp.sin(angles)
    widened = values.astype(F32)
    first, second = widened[..., :half_dim], widened[..., half_dim:]
    return jnp.concatenate(
        [first * cosine - second * sine, second * cosine + first * sine], -1
    ).astype(BF16)


def decode_attend(queries, new_keys, new_values, cached_keys, cached_values, lengths):
    rows, kv_heads, group_size, _ = queries.shape
    scale = HEAD_DIM**-0.5
    positions = lengths.astype(F32)
    q_rot = rotate(queries, positions[:, None, None])
    k_rot = rotate(new_keys, positions[:, None])
    span = cached_keys.shape[1]
    cache_k = cached_keys.reshape(rows, span, kv_heads, HEAD_DIM)
    cache_v = cached_values.reshape(rows, span, kv_heads, HEAD_DIM)
    old = jnp.einsum("rgjd,rlgd->rgjl", q_rot, cache_k, preferred_element_type=F32) * scale
    valid = jnp.arange(span, dtype=jnp.int32)[None, :] < lengths[:, None]
    old = jnp.where(valid[:, None, None, :], old, -jnp.inf)
    own = jnp.einsum("rgjd,rgd->rgj", q_rot, k_rot, preferred_element_type=F32) * scale
    top = jnp.maximum(jnp.max(old, axis=-1), own)
    old_weights = jnp.exp(old - top[..., None])
    own_weight = jnp.exp(own - top)
    total = jnp.sum(old_weights, axis=-1) + own_weight
    old_probs = (old_weights / total[..., None]).astype(BF16)
    own_prob = (own_weight / total).astype(BF16)
    mixed = jnp.einsum("rgjl,rlgd->rgjd", old_probs, cache_v, preferred_element_type=F32)
    mixed = mixed + own_prob.astype(F32)[..., None] * new_values.astype(F32)[:, :, None, :]
    return mixed.astype(BF16)


def shards(
    prefill_rows,
    decode_rows,
    norm_gain,
    w_query,
    w_key,
    w_value,
    w_out,
    prefix_keys,
    prefix_values,
    prefill_start,
    cache_keys,
    cache_values,
    cache_lengths,
):
    index = lax.axis_index("tensor")
    core, chip_x, chip_z = index & 1, (index >> 1) & 1, index >> 2
    rows = prefill_rows.shape[0]
    dec = decode_rows.shape[0]
    chips = 2 * RING
    half = rows // 2
    quarter = half // 2
    width = prefill_rows.shape[1]

    x0 = norm_rows(prefill_rows, norm_gain.reshape(width // 128, 128))
    x0, decode_rows, w_key, w_value = together(x0, decode_rows, w_key, w_value)
    dec_own = rms_norm(decode_rows, norm_gain)
    dec_rows = exchange(
        jnp.broadcast_to(dec_own[None], (chips, dec, width)).reshape(chips * dec, width)
    )
    kv_own = jnp.concatenate(
        [
            jnp.concatenate([w_key.T, w_value.T], 0),
            jnp.concatenate([prefix_keys.T, prefix_values.T], 0),
        ],
        1,
    )
    places = []
    for z_off, flip in ((0, 0), (0, 1), (1, 0), (3, 0), (1, 1), (3, 1), (2, 0), (2, 1)):
        places.append((((chip_z + z_off) % RING) * 2 + (chip_x ^ flip)) * 2 + core)
    start = prefill_start[0]
    spots = jnp.stack(places).astype(jnp.int32)
    positions = (start + spots[:, None] * rows + jnp.arange(rows, dtype=jnp.int32)[None]).reshape(-1)
    angles = positions.astype(F32)[:, None] * frequencies()
    cosine, sine = jnp.cos(angles), jnp.sin(angles)
    core_spec = core.reshape(1).astype(jnp.int32)
    spec = jnp.concatenate([prefill_start, spots])

    x1, x3, x2, wq_other, kv_other, w_out, dec_rows, cosine, sine, spec = together(
        side(x0),
        up(x0),
        down(x0),
        swap(w_query),
        swap(kv_own),
        w_out,
        dec_rows,
        cosine,
        sine,
        spec,
    )
    x7 = across(x1)
    some = quarter
    rest = rows - some
    by_up, by_down, by_side = add_up(
        [x1, x2, x3],
        [some + half, some + half, 2 * rest],
        [
            [(0, 0, 0, some), (2, 0, some, half)],
            [(0, 0, 0, some), (1, half, some, half)],
            [(1, some, 0, rest), (2, some, rest, rest)],
        ],
        24,
        "regroup",
    )
    from_down, from_up, from_side = up(by_up), down(by_down), side(by_side)
    x1, x2, x3, *_ = together(x1, x2, x3, by_up, by_down, by_side)
    weights = (w_query, wq_other, kv_own, kv_other)
    turned = 4 * rows
    q_near, kv_near, dec_qkv = project(
        [x0, x1, x2, x3, dec_rows],
        [(i, 0, rows) for i in range(4)] + [(4, 0, chips * dec)],
        turned,
        core_spec,
        weights,
        cosine,
        sine,
        0,
        "project_near",
    )
    mine = exchange(dec_qkv)
    wo_other = swap(w_out)
    from_down, from_up, from_side, x7, mine, kv_near, wo_other = together(
        from_down, from_up, from_side, x7, mine, kv_near, wo_other
    )
    q_far, kv_far = project(
        [from_down, from_up, from_side, x7],
        [(1, 0, some), (2, 0, rest), (0, 0, some), (2, rest, rest), (0, some, half), (1, some, half)]
        + [(3, 0, rows)],
        turned,
        core_spec,
        weights,
        cosine,
        sine,
        1,
        "project_far",
    )
    kv_near, kv_far = together(kv_near, kv_far)
    kv_near_other, kv_far_other = swap(kv_near), swap(kv_far)

    own, other = [kv_near, kv_far], [kv_near_other, kv_far_other]
    prefix = prefix_keys.shape[0]
    def cut(*sizes):
        ends = [sum(sizes[: i + 1]) for i in range(len(sizes))]
        return [(end - size, end) for size, end in zip(sizes, ends)]

    def attend_blocks(q, base, first, step, dec_attn, layout, extra, terms, name):
        return attend(
            spec,
            q,
            base,
            first,
            step,
            kv_own,
            kv_other,
            prefix,
            own,
            other,
            dec_attn,
            w_out,
            wo_other,
            layout,
            extra,
            terms,
            rows,
            name,
        )

    p4, p7 = attend_blocks(q_far, RING, 0, 3, None, cut(rows, rows), (), (), "attend_4_7")
    mine, q_far, p4, p7 = together(mine, q_far, p4, p7)
    r2, r1 = side(p4), across(p7)
    p5, p6 = attend_blocks(q_far, RING, 1, 1, None, cut(rows, rows), (), (), "attend_5_6")
    q_cols = 2 * w_query.shape[1]
    mine = mine.reshape(chips, dec, -1).transpose(1, 0, 2)
    dec_attn = decode_attend(
        mine[:, :, :q_cols].reshape(dec, chips, q_cols // HEAD_DIM, HEAD_DIM),
        mine[:, :, q_cols : q_cols + HEAD_DIM],
        mine[:, :, q_cols + HEAD_DIM :],
        cache_keys,
        cache_values,
        cache_lengths,
    )
    dec_attn = exchange(
        dec_attn.reshape(dec, chips, q_cols).transpose(1, 0, 2).reshape(chips * dec, q_cols)
    )
    q_near, p5, p6, r1, r2, dec_attn = together(q_near, p5, p6, r1, r2, dec_attn)
    r3_side, r3_down = side(p5), down(p6)
    p0, p1, p2, p3, pdec = attend_blocks(
        q_near,
        0,
        0,
        1,
        dec_attn,
        cut(*[rows] * 4, chips * dec),
        (1, 2),
        (r1, r2),
        "attend_near",
    )
    (p3,) = add_up([p3, r3_side, r3_down], [rows], [[(i, 0, 0, rows) for i in range(3)]], 56, "add_3")
    s1, s2, s3 = together(side(p1), up(p2), down(p3))
    dec_parts = exchange(pdec).reshape(chips, dec, width)
    decode_out = jnp.sum(dec_parts.astype(F32), axis=0).astype(BF16)
    (prefill_out,) = add_up(
        [p0, s1, s2, s3], [rows], [[(i, 0, 0, rows) for i in range(4)]], 24, "add_near"
    )
    return (prefill_out, decode_out)


def solution(mesh):
    in_specs = (
        P(("dp", "tensor"), None),
        P(("dp", "tensor"), None),
        P(),
        P(None, "tensor"),
        P(None, "tensor"),
        P(None, "tensor"),
        P("tensor", None),
        P("dp", "tensor"),
        P("dp", "tensor"),
        P("dp"),
        P(("dp", "tensor"), None, None),
        P(("dp", "tensor"), None, None),
        P(("dp", "tensor")),
    )
    out_specs = (P(("dp", "tensor"), None), P(("dp", "tensor"), None))
    return jax.shard_map(shards, mesh=mesh, in_specs=in_specs, out_specs=out_specs, check_vma=False)
```
